512 devices in a mesh: tm: 16 (over y, core), chan: 32 (over z, x).
Axes of the slice: x: 4, y: 8, z: 8, core: 2. Of those that a mesh axis runs over, the one named last changes fastest.
Arguments:
- records: bfloat16 [768, 16384], P('chan', 'tm'), may hold values from -40 to 40
- template_waves: bfloat16 [256, 12, 256], P('chan', None, 'tm'), may hold values from -11 to 11
- channel_lists: int32 [256, 12], replicated, may hold values from -1 to 767, as said below
- moveouts: int32 [256, 12], replicated, may hold values from 0 to 191
- owner_map: int32 [256, 1], replicated, may hold values from 0 to 31; in each aligned block of 8 rows (0 to 7, 8 to 15, ...) at most 2 rows name the same one
Outputs:
- stacks: float32 [2048, 16384], P('chan', 'tm')
The draws below stay inside these ranges and needn't reach their ends.
Inputs may be any that keep to these rules, and one draw needn't show every extreme that they name: `channel_lists`: template k lists n of 8 to 12 channels in slots 0 to n - 1, slot j holding (3 k + r + j) mod 768 with an offset r of 0 to 5 of its own; later slots are -1. Some template has r = 5 and n = 12. `owner_map`: among the templates of one block of 8 (equal k // 8) no owner is named more than 2 times.
All inputs are finite; a program needn't handle non-finite values.
Results may differ from the reference program's by a relative error of at most 0.0003.
Values may be sent and summed in bfloat16 or wider, within the bound.
No kernel may reach another device: no remote copies, remote signals or barrier semaphores. Data moves between devices by JAX's collectives and lax.ppermute only.
A program may use at most 64 MiB of HBM per device.

```python
import math
import jax
import jax.numpy as jnp
import numpy as np
from jax import lax

L = 256
SLOTS = 12
MAXMV = 192
TPL_DEV = 8
CHANNELS = 768
TEMPLATES = 256
SAMPLES = 16384
SCAP = 2
N_CHAN = 32


def draw_records(key, part):
    key = jax.random.fold_in(key, 11)
    key_noise, key_chan, key_env = jax.random.split(key, 3)
    noise = jnp.clip(jax.random.normal(key_noise, (CHANNELS, SAMPLES), jnp.float32), -4.0, 4.0)
    chan_scale = jnp.exp(jax.random.uniform(key_chan, (CHANNELS, 1), jnp.float32, -0.9, 0.9))
    envelope = jnp.exp(jax.random.uniform(key_env, (CHANNELS, SAMPLES // 32), jnp.float32, -0.8, 0.8))
    envelope = jnp.repeat(envelope, 32, axis=1)
    values = jnp.clip(noise * chan_scale * envelope, -40.0, 40.0)
    return values.astype(jnp.bfloat16)


def draw_template_waves(key, part):
    key = jax.random.fold_in(key, 23)
    key_noise, key_amp = jax.random.split(key, 2)
    noise = jnp.clip(jax.random.normal(key_noise, (TEMPLATES, SLOTS, L), jnp.float32), -4.0, 4.0)
    amplitude = jnp.exp(jax.random.uniform(key_amp, (TEMPLATES, SLOTS, 1), jnp.float32, -1.0, 1.0))
    taper = 0.5 + 0.5 * jnp.sin(jnp.pi * (jnp.arange(L, dtype=jnp.float32) + 0.5) / L)
    values = jnp.clip(noise * amplitude * taper[None, None, :], -11.0, 11.0)
    return values.astype(jnp.bfloat16)


def draw_channel_lists(key, part):
    key = jax.random.fold_in(key, 37)
    key_off, key_num, key_pick = jax.random.split(key, 3)
    offsets = jax.random.randint(key_off, (TEMPLATES,), 0, 6)
    counts = jax.random.randint(key_num, (TEMPLATES,), 8, 13)
    chosen = jax.random.randint(key_pick, (), 0, TEMPLATES)
    template_ids = jnp.arange(TEMPLATES, dtype=jnp.int32)
    offsets = jnp.where(template_ids == chosen, 5, offsets)
    counts = jnp.where(template_ids == chosen, 12, counts)
    slot_ids = jnp.arange(SLOTS, dtype=jnp.int32)
    listed = (3 * template_ids[:, None] + offsets[:, None] + slot_ids[None, :]) % CHANNELS
    listed = jnp.where(slot_ids[None, :] < counts[:, None], listed, -1)
    return listed.astype(jnp.int32)


def draw_moveouts(key, part):
    key = jax.random.fold_in(key, 41)
    key_vals, key_pick = jax.random.split(key, 2)
    values = jax.random.randint(key_vals, (TEMPLATES, SLOTS), 0, MAXMV)
    chosen = jax.random.randint(key_pick, (), 0, TEMPLATES * SLOTS)
    flat_ids = jnp.arange(TEMPLATES * SLOTS, dtype=jnp.int32).reshape(TEMPLATES, SLOTS)
    values = jnp.where(flat_ids == chosen, MAXMV - 1, values)
    return values.astype(jnp.int32)


def routed_block(own_key, own, number, rows, number_of, top, reach, slope):
    sequence = jax.random.permutation(own_key, number_of)
    packed, usual = shares(number_of, rows * top, reach, slope, True), shares(number_of, rows * top, reach, slope, False)
    places = jnp.arange(number_of)

    def named(sizes, rotation):
        used = int((sizes > 0).sum())
        fixed = max(1, used // 4)
        passed = fixed + (places - fixed + rotation * (used - fixed)) % max(1, number_of - fixed)
        return jnp.zeros((number_of,), jnp.int32).at[sequence[jnp.where(places < fixed, places, passed)]].set(jnp.asarray(sizes, jnp.int32))

    sizes = jnp.where(number % 4 == 0, named(packed, number // 4), named(usual, number - number // 4 - 1))
    mixed = jax.random.permutation(jax.random.fold_in(own, 3), number_of)
    source_of, receiver = mixed[0:number_of // 2 * 2:2], mixed[1:number_of // 2 * 2:2]
    slack = jnp.minimum(sizes[source_of] - 1, reach - sizes[receiver]) // 2
    slack = jnp.where((source_of == sequence[0]) | (receiver == sequence[0]) | (sizes[receiver] == 0), 0, jnp.maximum(slack, 0))
    passed = jax.random.randint(jax.random.fold_in(own, 4), (number_of // 2,), 0, 1 << 20) % (slack + 1)
    sizes = sizes.at[source_of].add(-passed).at[receiver].add(passed)
    labels = jnp.searchsorted(jnp.cumsum(sizes), jnp.arange(rows * top), side="right").astype(jnp.int32)
    table = labels.reshape(top, rows).T
    table = table[jax.random.permutation(jax.random.fold_in(own, 1), rows)]
    rotation = jax.random.randint(jax.random.fold_in(own, 2), (rows, 1), 0, top)
    return jnp.take_along_axis(table, (jnp.arange(top)[None, :] + rotation) % top, axis=1)


def shares(count, total, bound, skew, full):
    weights = [(1 << 20) // math.isqrt(grade ** skew) + 1 for grade in range(1, count + 1)]
    largest = bound if full else min(bound, max(-(-total // count), total * weights[0] // sum(weights)))
    least = 1 if total - largest >= count - 1 else 0
    given, surplus = [largest] + [least] * (count - 1), total - largest - least * (count - 1)
    while surplus > 0:
        candidates = [i for i in range(1, count) if given[i] < largest] or [i for i in range(1, count) if given[i] < bound]
        pool, budget = sum([weights[i] for i in candidates]), surplus
        for i in candidates:
            addition = min(bound - given[i], max(1, budget * weights[i] // pool), surplus)
            given[i] = given[i] + addition
            surplus = surplus - addition
    return np.array(given)


def setup_inputs(seed: int = 0) -> dict:
    arg_keys = jax.random.split(jax.random.key(seed), 6)
    records = draw_records(jax.random.fold_in(arg_keys[5], 71), 0)
    template_waves = draw_template_waves(jax.random.fold_in(arg_keys[5], 71), 0)
    channel_lists = draw_channel_lists(jax.random.fold_in(arg_keys[5], 71), 0)
    moveouts = draw_moveouts(jax.random.fold_in(arg_keys[5], 71), 0)
    owner_map_keys = jax.random.split(jax.random.fold_in(arg_keys[4], 1), TEMPLATES // TPL_DEV)
    owner_map_turns = jax.random.permutation(jax.random.fold_in(arg_keys[4], 3), TEMPLATES // TPL_DEV)
    owner_map = jax.vmap(lambda own, number: routed_block(jax.random.fold_in(arg_keys[4], 2), own, number, TPL_DEV, N_CHAN, 1, SCAP, 2))(owner_map_keys, owner_map_turns).reshape((TEMPLATES, 1))
    return dict(records=records, template_waves=template_waves, channel_lists=channel_lists, moveouts=moveouts, owner_map=owner_map)


def window_energy(squares, length_out, tap_count):
    block_len = 32
    blocks_n = length_out // block_len
    full_blocks = tap_count // block_len
    needed = (blocks_n + full_blocks + 1) * block_len
    if squares.shape[1] < needed:
        squares = jnp.pad(squares, ((0, 0), (0, needed - squares.shape[1])))
    else:
        squares = squares[:, :needed]
    row_count = squares.shape[0]
    blocks = squares.reshape(row_count, blocks_n + full_blocks + 1, block_len)
    inner_sum = jnp.cumsum(blocks, axis=2)
    before = inner_sum - blocks
    totals = inner_sum[:, :, block_len - 1:]
    energy = totals[:, :blocks_n] - before[:, :blocks_n]
    for offset in range(1, full_blocks):
        energy = energy + totals[:, offset:offset + blocks_n]
    energy = energy + before[:, full_blocks:full_blocks + blocks_n]
    return energy.reshape(row_count, blocks_n * block_len)

def reference(records, template_waves, channel_lists, moveouts, owner_map):
    signal = records.astype(jnp.float32)
    squared = signal * signal
    wrapped = jnp.concatenate([squared, squared[:, :L + 32]], axis=1)
    energy = window_energy(wrapped, SAMPLES, L)
    spectra = jnp.fft.rfft(signal, axis=1)
    sample_ids = jnp.arange(SAMPLES, dtype=jnp.int32)

    def one_template(operands):
        lists, shifts, shapes = operands
        is_valid = lists >= 0
        row_ids = jnp.where(is_valid, lists, 0).astype(jnp.int32)
        wave_f = shapes.astype(jnp.float32)
        wave_spec = jnp.fft.rfft(wave_f, n=SAMPLES, axis=1)
        corr = jnp.fft.irfft(spectra[row_ids] * jnp.conj(wave_spec), n=SAMPLES, axis=1)
        sample_idx = ((sample_ids[None, :] + shifts[:, None]) % SAMPLES).astype(jnp.int32)
        shifted = jnp.take_along_axis(corr, sample_idx, axis=1)
        window = jnp.take_along_axis(energy[row_ids], sample_idx, axis=1)
        wave_sq = lax.optimization_barrier(jnp.sum(wave_f * wave_f, axis=1))
        normed = shifted / jnp.sqrt(wave_sq[:, None] * window + 1e-06)
        normed = jnp.where(is_valid[:, None], normed, jnp.zeros_like(normed))
        return lax.optimization_barrier(jnp.sum(normed, axis=0))
    detect = lax.map(one_template, (channel_lists, moveouts, template_waves))
    owners = owner_map[:, 0].astype(jnp.int32)
    template_ids = jnp.arange(TEMPLATES, dtype=jnp.int32)
    block_of = template_ids // TPL_DEV
    earlier = (owners[None, :] == owners[:, None]) & (block_of[None, :] == block_of[:, None]) & (template_ids[None, :] < template_ids[:, None])
    slot_rank = lax.optimization_barrier(jnp.sum(earlier.astype(jnp.int32), axis=1)).astype(jnp.int32)
    target = ((owners * N_CHAN + block_of) * SCAP + slot_rank).astype(jnp.int32)
    result = jnp.zeros((N_CHAN * N_CHAN * SCAP, SAMPLES), detect.dtype).at[target].set(detect)
    return result
```

```python
import jax
import jax.numpy as jnp
from jax import lax
from jax.experimental import pallas as pl
from jax.experimental.pallas import tpu as pltpu
from jax.sharding import PartitionSpec as P

L = 256
SLOTS = 12
SPILL = 16
LANES = 128
ROWS = 16
HALO = 512
TPL = 8
CH = 24
SCAP = 2
F32 = jnp.float32
BF16 = jnp.bfloat16


def shift_pairs(count, steps):
    return [(source, (source + steps) % count) for source in range(count)]


def stack_kernel(total_chan, tab, rec, right, down, diag, waves, out, xs, xx, ee, pr, wr, we, sh):
    group = lax.axis_index("chan")
    rows_all = (CH + SPILL) * ROWS

    xs[...] = jnp.zeros_like(xs)
    for b in range(8):
        cut = slice(LANES * b, LANES * (b + 1))
        xs[pl.ds(b, CH, stride=ROWS), :] = rec[:, cut].astype(F32)
        xs[pl.ds(CH * ROWS + b, SPILL, stride=ROWS), :] = down[:, cut].astype(F32)
    for b in range(4):
        cut = slice(LANES * b, LANES * (b + 1))
        xs[pl.ds(8 + b, CH, stride=ROWS), :] = right[:, cut].astype(F32)
        xs[pl.ds(CH * ROWS + 8 + b, SPILL, stride=ROWS), :] = diag[:, cut].astype(F32)

    row_id = lax.broadcasted_iota(jnp.int32, (LANES, LANES), 0)
    lane_id = lax.broadcasted_iota(jnp.int32, (LANES, LANES), 1)
    lower = jnp.where(row_id >= lane_id, 1.0, 0.0).astype(BF16)
    upper = jnp.where(row_id < lane_id, 1.0, 0.0).astype(BF16)
    tri = jnp.concatenate([lower, upper], axis=1)
    ones_band = jnp.concatenate([tri, tri], axis=0)

    now = xs[pl.ds(0, rows_all), :]
    nxt = xs[pl.ds(1, rows_all), :]
    pair = jnp.concatenate([now, nxt], axis=1)
    xx[...] = pair.astype(BF16)
    square = pair * pair
    high = square.astype(BF16)
    low = (square - high.astype(F32)).astype(BF16)
    both = jnp.dot(high, ones_band, preferred_element_type=F32) + jnp.dot(
        low, ones_band, preferred_element_type=F32
    )
    pr[pl.ds(0, rows_all), :] = both[:, LANES:]
    ee[...] = both[:, :LANES] + pr[pl.ds(1, rows_all), :]

    wave_t = waves[...].astype(F32).T
    sample_id = lax.broadcasted_iota(jnp.int32, (L, L), 0)
    place_id = lax.broadcasted_iota(jnp.int32, (L, L), 1)
    same_half = (sample_id >= LANES) == (place_id >= LANES)
    mirrored = ((sample_id + place_id) & (LANES - 1)) == 0
    turn = jnp.where(same_half & mirrored, 1.0, 0.0).astype(BF16)
    turned = jnp.dot(wave_t.astype(BF16), turn, preferred_element_type=F32)
    wr[0] = turned[:, :LANES]
    wr[1] = turned[:, LANES:]
    we[...] = jnp.broadcast_to(jnp.sum(wave_t * wave_t, axis=1, keepdims=True), we.shape)

    out[...] = jnp.zeros_like(out)
    lane_row = lax.broadcasted_iota(jnp.int32, (TPL, LANES), 1)

    def circulant(p, half):
        row = wr[half, pl.ds(p, 1), :]
        full = jnp.broadcast_to(row, (LANES, LANES))
        return pltpu.roll(full, 0, 1, stride=1, stride_axis=0).astype(BF16)

    def one_template(k, carry):
        total = jnp.zeros((TPL, LANES), F32)
        for j in range(SLOTS):
            p = k * SLOTS + j
            listed = tab[k, j]
            valid = listed >= 0
            place = listed - group * CH
            place = jnp.where(place < 0, place + total_chan, place)
            place = jnp.where(valid, place, 0)
            start = pl.multiple_of(place * ROWS, ROWS)
            shift = tab[k, SLOTS + j]
            lanes, rows = shift & (LANES - 1), shift >> 7
            first, second = circulant(p, 0), circulant(p, 1)
            band = jnp.concatenate(
                [
                    jnp.concatenate([first * lower, first * upper], axis=1),
                    jnp.concatenate([second * lower, second * upper], axis=1),
                ],
                axis=0,
            )
            prod = jnp.dot(xx[pl.ds(start, ROWS), :], band, preferred_element_type=F32)
            corr = prod[:, :LANES] + pltpu.roll(prod[:, LANES:], ROWS - 1, 0)
            scale = we[pl.ds(p, 1), :] * ee[pl.ds(start, ROWS), :] + 1e-06
            normed = corr * lax.rsqrt(scale)
            sh[j] = pltpu.roll(normed, (LANES - lanes) & (LANES - 1), 1)
            here = sh[j, pl.ds(rows, TPL), :]
            after = sh[j, pl.ds(rows + 1, TPL), :]
            moved = jnp.where(lane_row < LANES - lanes, here, after)
            total = total + jnp.where(valid, moved, 0.0)
        owner = tab[k, 2 * SLOTS]
        rank = jnp.int32(0)
        for q in range(TPL):
            same = (tab[q, 2 * SLOTS] == owner) & (q < k)
            rank = rank + jnp.where(same, 1, 0)
        out[owner * SCAP + rank] = total
        return carry

    lax.fori_loop(0, TPL, one_template, 0)


def local(records, template_waves, channel_lists, moveouts, owner_map):
    ch_dev, t_dev = records.shape
    n_chan = lax.axis_size("chan")
    n_tm = lax.axis_size("tm")
    total_chan = ch_dev * n_chan
    group = lax.axis_index("chan")

    pairs_n = TPL * SLOTS
    own = template_waves.reshape(pairs_n, L // n_tm).T
    own = jnp.pad(own, ((0, 0), (0, LANES - pairs_n)))
    waves = lax.all_to_all(
        jnp.broadcast_to(own[None], (n_tm, L // n_tm, LANES)), "tm", 0, 0
    ).reshape(L, LANES)
    right = lax.ppermute(records[:, :HALO], "tm", shift_pairs(n_tm, -1))
    down = lax.ppermute(records[:SPILL], "chan", shift_pairs(n_chan, -1))
    across = [
        (t * n_chan + g, (t - 1) % n_tm * n_chan + (g - 1) % n_chan)
        for t in range(n_tm)
        for g in range(n_chan)
    ]
    diag = lax.ppermute(records[:SPILL, :HALO], ("tm", "chan"), across)
    table = jnp.concatenate([channel_lists, moveouts, owner_map], axis=1)
    table = lax.dynamic_slice_in_dim(table, group * TPL, TPL, 0)

    rows_all = (CH + SPILL) * ROWS
    vmem = pl.BlockSpec(memory_space=pltpu.VMEM)
    outgoing = pl.pallas_call(
        lambda *refs: stack_kernel(total_chan, *refs),
        out_shape=jax.ShapeDtypeStruct((n_chan * SCAP, TPL, LANES), F32),
        in_specs=[pl.BlockSpec(memory_space=pltpu.SMEM)] + [vmem] * 5,
        out_specs=vmem,
        scratch_shapes=[
            pltpu.VMEM((rows_all + 8, LANES), F32),
            pltpu.VMEM((rows_all, 2 * LANES), BF16),
            pltpu.VMEM((rows_all, LANES), F32),
            pltpu.VMEM((rows_all + 8, LANES), F32),
            pltpu.VMEM((2, LANES, LANES), F32),
            pltpu.VMEM((LANES, LANES), F32),
            pltpu.VMEM((SLOTS, ROWS, LANES), F32),
        ],
        compiler_params=pltpu.CompilerParams(vmem_limit_bytes=32 * 1024 * 1024),
    )(table, records, right, down, diag, waves)
    incoming = lax.all_to_all(
        outgoing.reshape(n_chan, SCAP, TPL, LANES), "chan", 0, 0
    )
    return incoming.reshape(n_chan * SCAP, t_dev)


def solution(mesh):
    in_specs = (P("chan", "tm"), P("chan", None, "tm"), P(), P(), P())
    out_specs = P("chan", "tm")
    return jax.shard_map(local, mesh=mesh, in_specs=in_specs, out_specs=out_specs, check_vma=False)
```

```python
import jax
import jax.numpy as jnp
from jax import lax
from jax.experimental import pallas as pl
from jax.experimental.pallas import tpu as pltpu
from jax.sharding import PartitionSpec as P

L = 256
SLOTS = 12
SPILL = 16
LANES = 128
ROWS = 16
HALO = 512
TPL = 8
CH = 24
SCAP = 2
PAIRS = TPL * SLOTS
ALL_ROWS = (CH + SPILL) * ROWS
F32 = jnp.float32
BF16 = jnp.bfloat16


def chunk_kernel(waves, out):
    rows = [waves[j].astype(F32) for j in range(SLOTS)]
    flat = jnp.concatenate(rows + [jnp.zeros((LANES - PAIRS, rows[0].shape[1]), F32)], axis=0)
    wide = jnp.concatenate([flat, jnp.zeros((LANES, LANES - flat.shape[1]), F32)], axis=1)
    turned = wide.T[: out.shape[1]].astype(BF16)
    for i in range(out.shape[0]):
        out[i] = turned


def frame_kernel(rec, right, below, xx, ee, xs, pr):
    for b in range(8):
        cut = slice(LANES * b, LANES * (b + 1))
        xs[pl.ds(b, CH, stride=ROWS), :] = rec[:, cut].astype(F32)
    for b in range(4):
        cut = slice(LANES * b, LANES * (b + 1))
        xs[pl.ds(8 + b, CH, stride=ROWS), :] = right[:, cut].astype(F32)
        xs[pl.ds(12 + b, CH + SPILL, stride=ROWS), :] = jnp.zeros((CH + SPILL, LANES), F32)
    for b in range(12):
        cut = slice(LANES * b, LANES * (b + 1))
        xs[pl.ds(CH * ROWS + b, SPILL, stride=ROWS), :] = below[:, cut].astype(F32)
    xs[pl.ds(ALL_ROWS, 8), :] = jnp.zeros((8, LANES), F32)

    row_id = lax.broadcasted_iota(jnp.int32, (LANES, LANES), 0)
    lane_id = lax.broadcasted_iota(jnp.int32, (LANES, LANES), 1)
    lower = jnp.where(row_id >= lane_id, 1.0, 0.0).astype(BF16)
    upper = jnp.where(row_id < lane_id, 1.0, 0.0).astype(BF16)
    tri = jnp.concatenate([lower, upper], axis=1)
    ones_band = jnp.concatenate([tri, tri], axis=0)

    now = xs[pl.ds(0, ALL_ROWS), :]
    nxt = xs[pl.ds(1, ALL_ROWS), :]
    pair = jnp.concatenate([now, nxt], axis=1)
    xx[...] = pair.astype(BF16)
    square = pair * pair
    high = square.astype(BF16)
    low = (square - high.astype(F32)).astype(BF16)
    both = jnp.dot(high, ones_band, preferred_element_type=F32) + jnp.dot(
        low, ones_band, preferred_element_type=F32
    )
    pr[pl.ds(0, ALL_ROWS), :] = both[:, LANES:]
    pr[pl.ds(ALL_ROWS, 8), :] = jnp.zeros((8, LANES), F32)
    ee[...] = both[:, :LANES] + pr[pl.ds(1, ALL_ROWS), :]


def stack_kernel(total_chan, lists, moves, owners, xx, ee, waves, out, wr, we, sh):
    group = lax.axis_index("chan")
    wave_t = waves[...].astype(F32).T
    sample_id = lax.broadcasted_iota(jnp.int32, (L, L), 0)
    place_id = lax.broadcasted_iota(jnp.int32, (L, L), 1)
    same_half = (sample_id >= LANES) == (place_id >= LANES)
    mirrored = ((sample_id + place_id) & (LANES - 1)) == 0
    turn = jnp.where(same_half & mirrored, 1.0, 0.0).astype(BF16)
    turned = jnp.dot(wave_t.astype(BF16), turn, preferred_element_type=F32)
    wr[0] = turned[:, :LANES]
    wr[1] = turned[:, LANES:]
    we[...] = jnp.broadcast_to(jnp.sum(wave_t * wave_t, axis=1, keepdims=True), we.shape)

    out[...] = jnp.zeros_like(out)
    lane_row = lax.broadcasted_iota(jnp.int32, (TPL, LANES), 1)
    row_id = lax.broadcasted_iota(jnp.int32, (LANES, LANES), 0)
    lane_id = lax.broadcasted_iota(jnp.int32, (LANES, LANES), 1)
    lower = jnp.where(row_id >= lane_id, 1.0, 0.0).astype(BF16)
    upper = jnp.where(row_id < lane_id, 1.0, 0.0).astype(BF16)

    def circulant(p, half):
        row = wr[half, pl.ds(p, 1), :]
        full = jnp.broadcast_to(row, (LANES, LANES)).astype(BF16)
        return pltpu.roll(full, 0, 1, stride=1, stride_axis=0)

    def one_template(k, carry):
        total = jnp.zeros((TPL, LANES), F32)
        tpl = group * TPL + k
        for j in range(SLOTS):
            p = j * TPL + k
            listed = lists[j, tpl]
            valid = listed >= 0
            place = listed - group * CH
            place = jnp.where(place < 0, place + total_chan, place)
            place = jnp.where(valid, place, 0)
            start = pl.multiple_of(place * ROWS, ROWS)
            shift = moves[j, tpl]
            lanes, rows = shift & (LANES - 1), shift >> 7
            first, second = circulant(p, 0), circulant(p, 1)
            band = jnp.concatenate(
                [
                    jnp.concatenate([first * lower, first * upper], axis=1),
                    jnp.concatenate([second * lower, second * upper], axis=1),
                ],
                axis=0,
            )
            prod = jnp.dot(xx[pl.ds(start, ROWS), :], band, preferred_element_type=F32)
            corr = prod[:, :LANES] + pltpu.roll(prod[:, LANES:], ROWS - 1, 0)
            scale = we[pl.ds(p, 1), :] * ee[pl.ds(start, ROWS), :] + 1e-06
            normed = corr * lax.rsqrt(scale)
            sh[j] = pltpu.roll(normed, (LANES - lanes) & (LANES - 1), 1)
            here = sh[j, pl.ds(rows, TPL), :]
            after = sh[j, pl.ds(rows + 1, TPL), :]
            moved = jnp.where(lane_row < LANES - lanes, here, after)
            total = total + jnp.where(valid, moved, 0.0)
        owner = owners[0, tpl]
        rank = jnp.int32(0)
        for q in range(TPL):
            same = (owners[0, group * TPL + q] == owner) & (q < k)
            rank = rank + jnp.where(same, 1, 0)
        out[owner * SCAP + rank] = total
        return carry

    lax.fori_loop(0, TPL, one_template, 0, unroll=True)


def shifted(value, axis, count):
    return lax.ppermute(value, axis, [(s, (s - 1) % count) for s in range(count)])


def gathered(chunks):
    return lax.all_to_all(chunks, "tm", 0, 0).reshape(L, LANES)


def local(records, template_waves, channel_lists, moveouts, owner_map):
    ch_dev, t_dev = records.shape
    n_chan = lax.axis_size("chan")
    n_tm = lax.axis_size("tm")
    vmem = pl.BlockSpec(memory_space=pltpu.VMEM)
    smem = pl.BlockSpec(memory_space=pltpu.SMEM)
    params = pltpu.CompilerParams(vmem_limit_bytes=24 * 1024 * 1024)

    chunks = pl.pallas_call(
        chunk_kernel,
        out_shape=jax.ShapeDtypeStruct((n_tm, L // n_tm, LANES), BF16),
        in_specs=[vmem],
        out_specs=vmem,
        compiler_params=params,
    )(jnp.transpose(template_waves, (1, 0, 2)))
    right = shifted(records[:, :HALO], "tm", n_tm)
    edge = jnp.concatenate([records[:SPILL], right[:SPILL]], axis=1)
    below = shifted(edge, "chan", n_chan)
    waves = gathered(chunks)
    frames, energy = pl.pallas_call(
        frame_kernel,
        out_shape=(
            jax.ShapeDtypeStruct((ALL_ROWS, 2 * LANES), BF16),
            jax.ShapeDtypeStruct((ALL_ROWS, LANES), F32),
        ),
        in_specs=[vmem] * 3,
        out_specs=(vmem, vmem),
        scratch_shapes=[
            pltpu.VMEM((ALL_ROWS + 8, LANES), F32),
            pltpu.VMEM((ALL_ROWS + 8, LANES), F32),
        ],
        compiler_params=params,
        cost_estimate=pl.CostEstimate(flops=200_000_000, bytes_accessed=1_000_000, transcendentals=0),
    )(records, right, below)
    outgoing = pl.pallas_call(
        lambda *refs: stack_kernel(ch_dev * n_chan, *refs),
        out_shape=jax.ShapeDtypeStruct((n_chan * SCAP, TPL, LANES), F32),
        in_specs=[smem] * 3 + [vmem] * 3,
        out_specs=vmem,
        scratch_shapes=[
            pltpu.VMEM((2, LANES, LANES), F32),
            pltpu.VMEM((LANES, LANES), F32),
            pltpu.VMEM((SLOTS, ROWS, LANES), F32),
        ],
        compiler_params=params,
    )(channel_lists.T, moveouts.T, owner_map.T, frames, energy, waves)
    incoming = lax.all_to_all(outgoing.reshape(n_chan, SCAP, TPL, LANES), "chan", 0, 0)
    return incoming.reshape(n_chan * SCAP, t_dev)


def solution(mesh):
    in_specs = (P("chan", "tm"), P("chan", None, "tm"), P(), P(), P())
    out_specs = P("chan", "tm")
    return jax.shard_map(local, mesh=mesh, in_specs=in_specs, out_specs=out_specs, check_vma=False)
```

```python
import jax
import jax.numpy as jnp
from jax import lax
from jax.experimental import pallas as pl
from jax.experimental.pallas import tpu as pltpu
from jax.sharding import PartitionSpec as P

L = 256
SLOTS = 12
SPILL = 16
LANES = 128
ROWS = 16
HALO = 512
TPL = 8
CH = 24
SCAP = 2
PAIRS = TPL * SLOTS
ALL_ROWS = (CH + SPILL) * ROWS
F32 = jnp.float32
BF16 = jnp.bfloat16


def chunk_kernel(waves, out):
    rows = [waves[j].astype(F32) for j in range(SLOTS)]
    flat = jnp.concatenate(rows + [jnp.zeros((LANES - PAIRS, rows[0].shape[1]), F32)], axis=0)
    wide = jnp.concatenate([flat, jnp.zeros((LANES, LANES - flat.shape[1]), F32)], axis=1)
    turned = wide.T[: out.shape[1]].astype(BF16)
    for i in range(out.shape[0]):
        out[i] = turned


def frame_kernel(rec, right, below, xx, ee, xs, pr):
    for b in range(8):
        cut = slice(LANES * b, LANES * (b + 1))
        xs[pl.ds(b, CH, stride=ROWS), :] = rec[:, cut].astype(F32)
    for b in range(4):
        cut = slice(LANES * b, LANES * (b + 1))
        xs[pl.ds(8 + b, CH, stride=ROWS), :] = right[:, cut].astype(F32)
        xs[pl.ds(12 + b, CH + SPILL, stride=ROWS), :] = jnp.zeros((CH + SPILL, LANES), F32)
    for b in range(12):
        cut = slice(LANES * b, LANES * (b + 1))
        xs[pl.ds(CH * ROWS + b, SPILL, stride=ROWS), :] = below[:, cut].astype(F32)
    xs[pl.ds(ALL_ROWS, 8), :] = jnp.zeros((8, LANES), F32)

    row_id = lax.broadcasted_iota(jnp.int32, (LANES, LANES), 0)
    lane_id = lax.broadcasted_iota(jnp.int32, (LANES, LANES), 1)
    lower = jnp.where(row_id >= lane_id, 1.0, 0.0).astype(BF16)
    upper = jnp.where(row_id < lane_id, 1.0, 0.0).astype(BF16)
    tri = jnp.concatenate([lower, upper], axis=1)
    ones_band = jnp.concatenate([tri, tri], axis=0)

    now = xs[pl.ds(0, ALL_ROWS), :]
    nxt = xs[pl.ds(1, ALL_ROWS), :]
    pair = jnp.concatenate([now, nxt], axis=1)
    xx[...] = pair.astype(BF16)
    square = pair * pair
    high = square.astype(BF16)
    low = (square - high.astype(F32)).astype(BF16)
    both = jnp.dot(high, ones_band, preferred_element_type=F32) + jnp.dot(
        low, ones_band, preferred_element_type=F32
    )
    pr[pl.ds(0, ALL_ROWS), :] = both[:, LANES:]
    pr[pl.ds(ALL_ROWS, 8), :] = jnp.zeros((8, LANES), F32)
    ee[...] = both[:, :LANES] + pr[pl.ds(1, ALL_ROWS), :]


def stack_kernel(total_chan, table, xx, ee, waves, out, wr, we, sh):
    group = lax.axis_index("chan")
    wave_t = waves[...].astype(F32).T
    sample_id = lax.broadcasted_iota(jnp.int32, (L, L), 0)
    place_id = lax.broadcasted_iota(jnp.int32, (L, L), 1)
    same_half = (sample_id >= LANES) == (place_id >= LANES)
    mirrored = ((sample_id + place_id) & (LANES - 1)) == 0
    turn = jnp.where(same_half & mirrored, 1.0, 0.0).astype(BF16)
    turned = jnp.dot(wave_t.astype(BF16), turn, preferred_element_type=F32)
    wr[0] = turned[:, :LANES]
    wr[1] = turned[:, LANES:]
    we[...] = jnp.broadcast_to(jnp.sum(wave_t * wave_t, axis=1, keepdims=True), we.shape)

    out[...] = jnp.zeros_like(out)
    lane_row = lax.broadcasted_iota(jnp.int32, (TPL, LANES), 1)
    row_id = lax.broadcasted_iota(jnp.int32, (LANES, LANES), 0)
    lane_id = lax.broadcasted_iota(jnp.int32, (LANES, LANES), 1)
    lower = jnp.where(row_id >= lane_id, 1.0, 0.0).astype(BF16)
    upper = jnp.where(row_id < lane_id, 1.0, 0.0).astype(BF16)

    def circulant(p, half):
        row = wr[half, pl.ds(p, 1), :]
        full = jnp.broadcast_to(row, (LANES, LANES)).astype(BF16)
        return pltpu.roll(full, 0, 1, stride=1, stride_axis=0)

    def one_template(k, carry):
        total = jnp.zeros((TPL, LANES), F32)
        for j in range(SLOTS):
            p = j * TPL + k
            listed = table[k, j]
            valid = listed >= 0
            place = listed - group * CH
            place = jnp.where(place < 0, place + total_chan, place)
            place = jnp.where(valid, place, 0)
            start = pl.multiple_of(place * ROWS, ROWS)
            shift = table[k, SLOTS + j]
            lanes, rows = shift & (LANES - 1), shift >> 7
            first, second = circulant(p, 0), circulant(p, 1)
            band = jnp.concatenate(
                [
                    jnp.concatenate([first * lower, first * upper], axis=1),
                    jnp.concatenate([second * lower, second * upper], axis=1),
                ],
                axis=0,
            )
            prod = jnp.dot(xx[pl.ds(start, ROWS), :], band, preferred_element_type=F32)
            corr = prod[:, :LANES] + pltpu.roll(prod[:, LANES:], ROWS - 1, 0)
            scale = we[pl.ds(p, 1), :] * ee[pl.ds(start, ROWS), :] + 1e-06
            normed = corr * lax.rsqrt(scale)
            sh[j] = pltpu.roll(normed, (LANES - lanes) & (LANES - 1), 1)
            here = sh[j, pl.ds(rows, TPL), :]
            after = sh[j, pl.ds(rows + 1, TPL), :]
            moved = jnp.where(lane_row < LANES - lanes, here, after)
            total = total + jnp.where(valid, moved, 0.0)
        owner = table[k, 2 * SLOTS]
        rank = jnp.int32(0)
        for q in range(TPL):
            same = (table[q, 2 * SLOTS] == owner) & (q < k)
            rank = rank + jnp.where(same, 1, 0)
        out[owner * SCAP + rank] = total
        return carry

    lax.fori_loop(0, TPL, one_template, 0, unroll=True)


def shifted(value, axis, count):
    return lax.ppermute(value, axis, [(s, (s - 1) % count) for s in range(count)])


def gathered(chunks):
    return lax.all_to_all(chunks, "tm", 0, 0).reshape(L, LANES)


def local(records, template_waves, channel_lists, moveouts, owner_map):
    ch_dev, t_dev = records.shape
    n_chan = lax.axis_size("chan")
    n_tm = lax.axis_size("tm")
    vmem = pl.BlockSpec(memory_space=pltpu.VMEM)
    smem = pl.BlockSpec(memory_space=pltpu.SMEM)
    params = pltpu.CompilerParams(vmem_limit_bytes=24 * 1024 * 1024)

    chunks = pl.pallas_call(
        chunk_kernel,
        out_shape=jax.ShapeDtypeStruct((n_tm, L // n_tm, LANES), BF16),
        in_specs=[vmem],
        out_specs=vmem,
        compiler_params=params,
    )(jnp.transpose(template_waves, (1, 0, 2)))
    right = shifted(records[:, :HALO], "tm", n_tm)
    edge = jnp.concatenate([records[:SPILL], right[:SPILL]], axis=1)
    below = shifted(edge, "chan", n_chan)
    waves = gathered(chunks)
    table = jnp.concatenate([channel_lists, moveouts, owner_map], axis=1)
    table = lax.dynamic_slice_in_dim(table, lax.axis_index("chan") * TPL, TPL, 0)
    frames, energy = pl.pallas_call(
        frame_kernel,
        out_shape=(
            jax.ShapeDtypeStruct((ALL_ROWS, 2 * LANES), BF16),
            jax.ShapeDtypeStruct((ALL_ROWS, LANES), F32),
        ),
        in_specs=[vmem] * 3,
        out_specs=(vmem, vmem),
        scratch_shapes=[
            pltpu.VMEM((ALL_ROWS + 8, LANES), F32),
            pltpu.VMEM((ALL_ROWS + 8, LANES), F32),
        ],
        compiler_params=params,
        cost_estimate=pl.CostEstimate(flops=200_000_000, bytes_accessed=1_000_000, transcendentals=0),
    )(records, right, below)
    outgoing = pl.pallas_call(
        lambda *refs: stack_kernel(ch_dev * n_chan, *refs),
        out_shape=jax.ShapeDtypeStruct((n_chan * SCAP, TPL, LANES), F32),
        in_specs=[smem] + [vmem] * 3,
        out_specs=vmem,
        scratch_shapes=[
            pltpu.VMEM((2, LANES, LANES), F32),
            pltpu.VMEM((LANES, LANES), F32),
            pltpu.VMEM((SLOTS, ROWS, LANES), F32),
        ],
        compiler_params=params,
    )(table, frames, energy, waves)
    incoming = lax.all_to_all(outgoing.reshape(n_chan, SCAP, TPL, LANES), "chan", 0, 0)
    return incoming.reshape(n_chan * SCAP, t_dev)


def solution(mesh):
    in_specs = (P("chan", "tm"), P("chan", None, "tm"), P(), P(), P())
    out_specs = P("chan", "tm")
    return jax.shard_map(local, mesh=mesh, in_specs=in_specs, out_specs=out_specs, check_vma=False)
```

```python
import jax
import jax.numpy as jnp
from jax import lax
from jax.experimental import pallas as pl
from jax.experimental.pallas import tpu as pltpu
from jax.sharding import PartitionSpec as P

L = 256
SLOTS = 12
SPILL = 16
LANES = 128
ROWS = 16
HALO = 512
TPL = 8
CH = 24
SCAP = 2
PAIRS = TPL * SLOTS
FROM = 16
F32 = jnp.float32
BF16 = jnp.bfloat16


def chunk_kernel(waves, out):
    rows = [waves[j].astype(F32) for j in range(SLOTS)]
    flat = jnp.concatenate(rows + [jnp.zeros((LANES - PAIRS, rows[0].shape[1]), F32)], axis=0)
    wide = jnp.concatenate([flat, jnp.zeros((LANES, LANES - flat.shape[1]), F32)], axis=1)
    turned = wide.T[: out.shape[1]]
    last = out.shape[1] - 1
    turned = jnp.concatenate([turned[last - i : last - i + 1] for i in range(last + 1)], axis=0).astype(BF16)
    for i in range(out.shape[0]):
        out[i] = turned


def triangles():
    row_id = lax.broadcasted_iota(jnp.int32, (LANES, LANES), 0)
    lane_id = lax.broadcasted_iota(jnp.int32, (LANES, LANES), 1)
    lower = jnp.where(row_id >= lane_id, 1.0, 0.0).astype(BF16)
    upper = jnp.where(row_id < lane_id, 1.0, 0.0).astype(BF16)
    return lower, upper


def frame_pairs(xs, pr, rows):
    tri = jnp.concatenate(triangles(), axis=1)
    ones_band = jnp.concatenate([tri, tri], axis=0)
    pair = jnp.concatenate([xs[pl.ds(0, rows), :], xs[pl.ds(1, rows), :]], axis=1)
    square = pair * pair
    high = square.astype(BF16)
    low = (square - high.astype(F32)).astype(BF16)
    both = jnp.dot(high, ones_band, preferred_element_type=F32) + jnp.dot(
        low, ones_band, preferred_element_type=F32
    )
    pr[pl.ds(0, rows), :] = both[:, LANES:]
    pr[pl.ds(rows, 8), :] = jnp.zeros((8, LANES), F32)
    return pair.astype(BF16), both[:, :LANES] + pr[pl.ds(1, rows), :]


def frame_kernel(rec, right, xx, ee, xs, pr):
    for b in range(12):
        part, at = (rec, b) if b < 8 else (right, b - 8)
        xs[pl.ds(b, CH, stride=ROWS), :] = part[:, LANES * at : LANES * (at + 1)].astype(F32)
    for b in range(12, ROWS):
        xs[pl.ds(b, CH, stride=ROWS), :] = jnp.zeros((CH, LANES), F32)
    xs[pl.ds(CH * ROWS, 8), :] = jnp.zeros((8, LANES), F32)
    xx[...], ee[...] = frame_pairs(xs, pr, CH * ROWS)


def own_slots(k):
    return min(SLOTS, max(0, CH - 5 - 3 * k))


def stacked(table, k, slots, first_row, total_chan, xx, ee, wr, we, sh):
    group = lax.axis_index("chan")
    lower, upper = triangles()
    lane_row = lax.broadcasted_iota(jnp.int32, (TPL, LANES), 1)

    def circulant(p, half):
        row = wr[half, pl.ds(p, 1), :]
        full = jnp.broadcast_to(row, (LANES, LANES)).astype(BF16)
        return pltpu.roll(full, 1, 1, stride=1, stride_axis=0)

    total = jnp.zeros((TPL, LANES), F32)
    for j in slots:
        p = j * TPL + k
        listed = table[k, j]
        valid = listed >= 0
        place = listed - group * CH
        place = jnp.where(place < 0, place + total_chan, place) - first_row
        place = jnp.where(valid, place, 0)
        start = pl.multiple_of(place * ROWS, ROWS)
        shift = table[k, SLOTS + j]
        lanes, rows = shift & (LANES - 1), shift >> 7
        first, second = circulant(p, 0), circulant(p, 1)
        band = jnp.concatenate(
            [
                jnp.concatenate([first * lower, first * upper], axis=1),
                jnp.concatenate([second * lower, second * upper], axis=1),
            ],
            axis=0,
        )
        prod = jnp.dot(xx[pl.ds(start, ROWS), :], band, preferred_element_type=F32)
        corr = prod[:, :LANES] + pltpu.roll(prod[:, LANES:], ROWS - 1, 0)
        scale = we[pl.ds(p, 1), :] * ee[pl.ds(start, ROWS), :] + 1e-06
        normed = corr * lax.rsqrt(scale)
        sh[j] = pltpu.roll(normed, (LANES - lanes) & (LANES - 1), 1)
        here = sh[j, pl.ds(rows, TPL), :]
        after = sh[j, pl.ds(rows + 1, TPL), :]
        moved = jnp.where(lane_row < LANES - lanes, here, after)
        total = total + jnp.where(valid, moved, 0.0)
    return total


def own_kernel(total_chan, table_v, xx, ee, waves, part, wr, we, sh, table, sem):
    copy = pltpu.make_async_copy(table_v, table, sem)
    copy.start()
    order = [h + i for h in (0, LANES) for i in reversed(range(0, LANES, ROWS))]
    wave_t = jnp.concatenate([waves[pl.ds(i, ROWS), :].astype(F32) for i in order], axis=0).T
    wr[0] = wave_t[:, :LANES]
    wr[1] = wave_t[:, LANES:]
    we[...] = jnp.broadcast_to(jnp.sum(wave_t * wave_t, axis=1, keepdims=True), we.shape)
    copy.wait()
    for k in range(TPL):
        part[k] = stacked(table, k, range(own_slots(k)), 0, total_chan, xx, ee, wr, we, sh)


def rest_kernel(total_chan, table_v, own_xx, own_ee, below, part, wr, we, out, xs, pr, xx, ee, sh, table, sem):
    copy = pltpu.make_async_copy(table_v, table, sem)
    copy.start()
    for b in range(12):
        xs[pl.ds(b, SPILL, stride=ROWS), :] = below[:, LANES * b : LANES * (b + 1)].astype(F32)
    for b in range(12, ROWS):
        xs[pl.ds(b, SPILL, stride=ROWS), :] = jnp.zeros((SPILL, LANES), F32)
    xs[pl.ds(SPILL * ROWS, 8), :] = jnp.zeros((8, LANES), F32)
    kept = (CH - FROM) * ROWS
    xx[pl.ds(0, kept), :] = own_xx[pl.ds(FROM * ROWS, kept), :]
    ee[pl.ds(0, kept), :] = own_ee[pl.ds(FROM * ROWS, kept), :]
    pairs, energy = frame_pairs(xs, pr, SPILL * ROWS)
    xx[pl.ds(kept, SPILL * ROWS), :] = pairs
    ee[pl.ds(kept, SPILL * ROWS), :] = energy

    out[...] = jnp.zeros_like(out)
    copy.wait()
    for k in range(TPL):
        slots = range(own_slots(k), SLOTS)
        total = part[k] + stacked(table, k, slots, FROM, total_chan, xx, ee, wr, we, sh)
        owner = table[k, 2 * SLOTS]
        rank = jnp.int32(0)
        for q in range(k):
            rank = rank + jnp.where(table[q, 2 * SLOTS] == owner, 1, 0)
        out[owner * SCAP + rank] = total


def shifted(value, axis, count):
    return lax.ppermute(value, axis, [(s, (s - 1) % count) for s in range(count)])


def gathered(chunks):
    return lax.all_to_all(chunks, "tm", 0, 0).reshape(L, LANES)


def local(records, template_waves, channel_lists, moveouts, owner_map):
    ch_dev, t_dev = records.shape
    n_chan = lax.axis_size("chan")
    n_tm = lax.axis_size("tm")
    vmem = pl.BlockSpec(memory_space=pltpu.VMEM)
    params = pltpu.CompilerParams(vmem_limit_bytes=24 * 1024 * 1024)

    chunks = pl.pallas_call(
        chunk_kernel,
        out_shape=jax.ShapeDtypeStruct((n_tm, L // n_tm, LANES), BF16),
        in_specs=[vmem],
        out_specs=vmem,
        compiler_params=params,
    )(jnp.transpose(template_waves, (1, 0, 2)))
    right = shifted(records, "tm", n_tm)
    edge = jnp.concatenate([records[:SPILL], right[:SPILL, :HALO]], axis=1)
    lists, shifts, owners, edge = lax.optimization_barrier((channel_lists, moveouts, owner_map, edge))
    below = shifted(edge, "chan", n_chan)
    table = jnp.concatenate([lists, shifts, owners], axis=1)
    table = lax.dynamic_slice_in_dim(table, lax.axis_index("chan") * TPL, TPL, 0)
    waves = gathered(chunks)
    scalars = [pltpu.SMEM((TPL, 2 * SLOTS + 1), jnp.int32), pltpu.SemaphoreType.DMA]

    def scratch(*shape):
        return pltpu.VMEM(shape, F32)

    frames, energy = pl.pallas_call(
        frame_kernel,
        out_shape=(
            jax.ShapeDtypeStruct((CH * ROWS, 2 * LANES), BF16),
            jax.ShapeDtypeStruct((CH * ROWS, LANES), F32),
        ),
        in_specs=[vmem] * 2,
        out_specs=(vmem, vmem),
        scratch_shapes=[scratch(CH * ROWS + 8, LANES)] * 2,
        compiler_params=params,
        cost_estimate=pl.CostEstimate(flops=200_000_000, bytes_accessed=1_000_000, transcendentals=0),
    )(records, right)
    part, rows_w, energy_w = pl.pallas_call(
        lambda *refs: own_kernel(ch_dev * n_chan, *refs),
        out_shape=(
            jax.ShapeDtypeStruct((TPL, TPL, LANES), F32),
            jax.ShapeDtypeStruct((2, LANES, LANES), F32),
            jax.ShapeDtypeStruct((LANES, LANES), F32),
        ),
        in_specs=[vmem] * 4,
        out_specs=(vmem,) * 3,
        scratch_shapes=[scratch(SLOTS, ROWS, LANES)] + scalars,
        compiler_params=params,
        cost_estimate=pl.CostEstimate(flops=1_000_000_000, bytes_accessed=1_000_000, transcendentals=0),
    )(table, frames, energy, waves)
    late_rows = (CH - FROM + SPILL) * ROWS
    outgoing = pl.pallas_call(
        lambda *refs: rest_kernel(ch_dev * n_chan, *refs),
        out_shape=jax.ShapeDtypeStruct((n_chan * SCAP, TPL, LANES), F32),
        in_specs=[vmem] * 7,
        out_specs=vmem,
        scratch_shapes=[
            scratch(SPILL * ROWS + 8, LANES),
            scratch(SPILL * ROWS + 8, LANES),
            pltpu.VMEM((late_rows, 2 * LANES), BF16),
            scratch(late_rows, LANES),
            scratch(SLOTS, ROWS, LANES),
        ]
        + scalars,
        compiler_params=params,
    )(table, frames, energy, below, part, rows_w, energy_w)
    incoming = lax.all_to_all(outgoing.reshape(n_chan, SCAP, TPL, LANES), "chan", 0, 0)
    return incoming.reshape(n_chan * SCAP, t_dev)


def solution(mesh):
    in_specs = (P("chan", "tm"), P("chan", None, "tm"), P(), P(), P())
    out_specs = P("chan", "tm")
    return jax.shard_map(local, mesh=mesh, in_specs=in_specs, out_specs=out_specs, check_vma=False)
```

```python
import jax
import jax.numpy as jnp
from jax import lax
from jax.experimental import pallas as pl
from jax.experimental.pallas import tpu as pltpu
from jax.sharding import PartitionSpec as P

L = 256
SLOTS = 12
SPILL = 16
LANES = 128
ROWS = 16
HALO = 512
TPL = 8
CH = 24
SCAP = 2
PAIRS = TPL * SLOTS
FROM = 16
F32 = jnp.float32
BF16 = jnp.bfloat16


def chunk_kernel(waves, out):
    rows = [waves[j].astype(F32) for j in range(SLOTS)]
    flat = jnp.concatenate(rows + [jnp.zeros((LANES - PAIRS, rows[0].shape[1]), F32)], axis=0)
    wide = jnp.concatenate([flat, jnp.zeros((LANES, LANES - flat.shape[1]), F32)], axis=1)
    turned = wide.T[: out.shape[1]]
    last = out.shape[1] - 1
    turned = jnp.concatenate([turned[last - i : last - i + 1] for i in range(last + 1)], axis=0).astype(BF16)
    for i in range(out.shape[0]):
        out[i] = turned


def triangles():
    row_id = lax.broadcasted_iota(jnp.int32, (LANES, LANES), 0)
    lane_id = lax.broadcasted_iota(jnp.int32, (LANES, LANES), 1)
    lower = jnp.where(row_id >= lane_id, 1.0, 0.0).astype(BF16)
    upper = jnp.where(row_id < lane_id, 1.0, 0.0).astype(BF16)
    return lower, upper


def frame_pairs(xs, pr, rows):
    tri = jnp.concatenate(triangles(), axis=1)
    ones_band = jnp.concatenate([tri, tri], axis=0)
    pair = jnp.concatenate([xs[pl.ds(0, rows), :], xs[pl.ds(1, rows), :]], axis=1)
    square = pair * pair
    high = square.astype(BF16)
    low = (square - high.astype(F32)).astype(BF16)
    both = jnp.dot(high, ones_band, preferred_element_type=F32) + jnp.dot(
        low, ones_band, preferred_element_type=F32
    )
    pr[pl.ds(0, rows), :] = both[:, LANES:]
    pr[pl.ds(rows, 8), :] = jnp.zeros((8, LANES), F32)
    return pair.astype(BF16), both[:, :LANES] + pr[pl.ds(1, rows), :]


def frame_kernel(rec, right, xx, ee, xs, pr):
    for b in range(12):
        part, at = (rec, b) if b < 8 else (right, b - 8)
        xs[pl.ds(b, CH, stride=ROWS), :] = part[:, LANES * at : LANES * (at + 1)].astype(F32)
    for b in range(12, ROWS):
        xs[pl.ds(b, CH, stride=ROWS), :] = jnp.zeros((CH, LANES), F32)
    xs[pl.ds(CH * ROWS, 8), :] = jnp.zeros((8, LANES), F32)
    xx[...], ee[...] = frame_pairs(xs, pr, CH * ROWS)


def own_slots(k):
    return min(SLOTS, max(0, CH - 5 - 3 * k))


def stacked(table, k, slots, first_row, total_chan, xx, ee, wr, we, sh):
    group = lax.axis_index("chan")
    lower, upper = triangles()
    lane_row = lax.broadcasted_iota(jnp.int32, (TPL, LANES), 1)

    def circulant(p, half):
        row = wr[half, pl.ds(p, 1), :]
        full = jnp.broadcast_to(row, (LANES, LANES)).astype(BF16)
        return pltpu.roll(full, 1, 1, stride=1, stride_axis=0)

    total = jnp.zeros((TPL, LANES), F32)
    for j in slots:
        p = j * TPL + k
        listed = table[k, j]
        valid = listed >= 0
        place = listed - group * CH
        place = jnp.where(place < 0, place + total_chan, place) - first_row
        place = jnp.where(valid, place, 0)
        start = pl.multiple_of(place * ROWS, ROWS)
        shift = table[k, SLOTS + j]
        lanes, rows = shift & (LANES - 1), shift >> 7
        first, second = circulant(p, 0), circulant(p, 1)
        band = jnp.concatenate(
            [
                jnp.concatenate([first * lower, first * upper], axis=1),
                jnp.concatenate([second * lower, second * upper], axis=1),
            ],
            axis=0,
        )
        prod = jnp.dot(xx[pl.ds(start, ROWS), :], band, preferred_element_type=F32)
        corr = prod[:, :LANES] + pltpu.roll(prod[:, LANES:], ROWS - 1, 0)
        scale = we[pl.ds(p, 1), :] * ee[pl.ds(start, ROWS), :] + 1e-06
        normed = corr * lax.rsqrt(scale)
        sh[j] = pltpu.roll(normed, (LANES - lanes) & (LANES - 1), 1)
        here = sh[j, pl.ds(rows, TPL), :]
        after = sh[j, pl.ds(rows + 1, TPL), :]
        moved = jnp.where(lane_row < LANES - lanes, here, after)
        total = total + jnp.where(valid, moved, 0.0)
    return total


def own_kernel(total_chan, table_v, xx, ee, waves, part, wr, we, sh, table, sem):
    copy = pltpu.make_async_copy(table_v, table, sem)
    copy.start()
    order = [h + i for h in (0, LANES) for i in reversed(range(0, LANES, ROWS))]
    wave_t = jnp.concatenate([waves[pl.ds(i, ROWS), :].astype(F32) for i in order], axis=0).T
    wr[0] = wave_t[:, :LANES]
    wr[1] = wave_t[:, LANES:]
    we[...] = jnp.broadcast_to(jnp.sum(wave_t * wave_t, axis=1, keepdims=True), we.shape)
    copy.wait()
    for k in range(TPL):
        part[k] = stacked(table, k, range(own_slots(k)), 0, total_chan, xx, ee, wr, we, sh)


def rest_kernel(total_chan, table_v, own_xx, own_ee, below, part, wr, we, out, xs, pr, xx, ee, sh, table, sem):
    copy = pltpu.make_async_copy(table_v, table, sem)
    copy.start()
    for b in range(12):
        xs[pl.ds(b, SPILL, stride=ROWS), :] = below[:, LANES * b : LANES * (b + 1)].astype(F32)
    for b in range(12, ROWS):
        xs[pl.ds(b, SPILL, stride=ROWS), :] = jnp.zeros((SPILL, LANES), F32)
    xs[pl.ds(SPILL * ROWS, 8), :] = jnp.zeros((8, LANES), F32)
    kept = (CH - FROM) * ROWS
    xx[pl.ds(0, kept), :] = own_xx[pl.ds(FROM * ROWS, kept), :]
    ee[pl.ds(0, kept), :] = own_ee[pl.ds(FROM * ROWS, kept), :]
    pairs, energy = frame_pairs(xs, pr, SPILL * ROWS)
    xx[pl.ds(kept, SPILL * ROWS), :] = pairs
    ee[pl.ds(kept, SPILL * ROWS), :] = energy

    out[...] = jnp.zeros_like(out)
    copy.wait()
    for k in range(TPL):
        slots = range(own_slots(k), SLOTS)
        total = part[k] + stacked(table, k, slots, FROM, total_chan, xx, ee, wr, we, sh)
        owner = table[k, 2 * SLOTS]
        rank = jnp.int32(0)
        for q in range(k):
            rank = rank + jnp.where(table[q, 2 * SLOTS] == owner, 1, 0)
        out[(out.shape[0] // SCAP - 1 - owner) * SCAP + rank] = total


def shifted(value, axis, count):
    return lax.ppermute(value, axis, [(s, (s - 1) % count) for s in range(count)])


def gathered(chunks):
    return lax.all_to_all(chunks, "tm", 0, 0).reshape(L, LANES)


def local(records, template_waves, channel_lists, moveouts, owner_map):
    ch_dev, t_dev = records.shape
    n_chan = lax.axis_size("chan")
    n_tm = lax.axis_size("tm")
    vmem = pl.BlockSpec(memory_space=pltpu.VMEM)
    params = pltpu.CompilerParams(vmem_limit_bytes=24 * 1024 * 1024)

    chunks = pl.pallas_call(
        chunk_kernel,
        out_shape=jax.ShapeDtypeStruct((n_tm, L // n_tm, LANES), BF16),
        in_specs=[vmem],
        out_specs=vmem,
        compiler_params=params,
    )(jnp.transpose(template_waves, (1, 0, 2)))
    right = shifted(records, "tm", n_tm)
    edge = jnp.concatenate([records[:SPILL], right[:SPILL, :HALO]], axis=1)
    lists, shifts, owners, edge = lax.optimization_barrier((channel_lists, moveouts, owner_map, edge))
    below = shifted(edge, "chan", n_chan)
    table = jnp.concatenate([lists, shifts, owners], axis=1)
    table = lax.dynamic_slice_in_dim(table, lax.axis_index("chan") * TPL, TPL, 0)
    waves = gathered(chunks)
    scalars = [pltpu.SMEM((TPL, 2 * SLOTS + 1), jnp.int32), pltpu.SemaphoreType.DMA]

    def scratch(*shape):
        return pltpu.VMEM(shape, F32)

    frames, energy = pl.pallas_call(
        frame_kernel,
        out_shape=(
            jax.ShapeDtypeStruct((CH * ROWS, 2 * LANES), BF16),
            jax.ShapeDtypeStruct((CH * ROWS, LANES), F32),
        ),
        in_specs=[vmem] * 2,
        out_specs=(vmem, vmem),
        scratch_shapes=[scratch(CH * ROWS + 8, LANES)] * 2,
        compiler_params=params,
        cost_estimate=pl.CostEstimate(flops=200_000_000, bytes_accessed=1_000_000, transcendentals=0),
    )(records, right)
    part, rows_w, energy_w = pl.pallas_call(
        lambda *refs: own_kernel(ch_dev * n_chan, *refs),
        out_shape=(
            jax.ShapeDtypeStruct((TPL, TPL, LANES), F32),
            jax.ShapeDtypeStruct((2, LANES, LANES), F32),
            jax.ShapeDtypeStruct((LANES, LANES), F32),
        ),
        in_specs=[vmem] * 4,
        out_specs=(vmem,) * 3,
        scratch_shapes=[scratch(SLOTS, ROWS, LANES)] + scalars,
        compiler_params=params,
        cost_estimate=pl.CostEstimate(flops=1_000_000_000, bytes_accessed=1_000_000, transcendentals=0),
    )(table, frames, energy, waves)
    late_rows = (CH - FROM + SPILL) * ROWS
    outgoing = pl.pallas_call(
        lambda *refs: rest_kernel(ch_dev * n_chan, *refs),
        out_shape=jax.ShapeDtypeStruct((n_chan * SCAP, TPL, LANES), F32),
        in_specs=[vmem] * 7,
        out_specs=vmem,
        scratch_shapes=[
            scratch(SPILL * ROWS + 8, LANES),
            scratch(SPILL * ROWS + 8, LANES),
            pltpu.VMEM((late_rows, 2 * LANES), BF16),
            scratch(late_rows, LANES),
            scratch(SLOTS, ROWS, LANES),
        ]
        + scalars,
        compiler_params=params,
    )(table, frames, energy, below, part, rows_w, energy_w)
    incoming = lax.all_to_all(
        outgoing.reshape(n_chan, SCAP, TPL, LANES),
        "chan",
        0,
        0,
        axis_index_groups=[list(reversed(range(n_chan)))],
    )[::-1]
    return incoming.reshape(n_chan * SCAP, t_dev)


def solution(mesh):
    in_specs = (P("chan", "tm"), P("chan", None, "tm"), P(), P(), P())
    out_specs = P("chan", "tm")
    return jax.shard_map(local, mesh=mesh, in_specs=in_specs, out_specs=out_specs, check_vma=False)
```

```python
import jax
import jax.numpy as jnp
from jax import lax
from jax.experimental import pallas as pl
from jax.experimental.pallas import tpu as pltpu
from jax.sharding import PartitionSpec as P

L = 256
SLOTS = 12
SPILL = 16
LANES = 128
ROWS = 16
HALO = 512
TPL = 8
CH = 24
SCAP = 2
PAIRS = TPL * SLOTS
FROM = 16
RING = [(15 + i) % 16 for i in range(16)]
F32 = jnp.float32
BF16 = jnp.bfloat16


def chunk_kernel(waves, out):
    rows = [waves[j].astype(F32) for j in range(SLOTS)]
    flat = jnp.concatenate(rows + [jnp.zeros((LANES - PAIRS, rows[0].shape[1]), F32)], axis=0)
    wide = jnp.concatenate([flat, jnp.zeros((LANES, LANES - flat.shape[1]), F32)], axis=1)
    turned = wide.T[: out.shape[1]]
    last = out.shape[1] - 1
    turned = jnp.concatenate([turned[last - i : last - i + 1] for i in range(last + 1)], axis=0).astype(BF16)
    for i in range(out.shape[0]):
        out[i] = turned


def triangles():
    row_id = lax.broadcasted_iota(jnp.int32, (LANES, LANES), 0)
    lane_id = lax.broadcasted_iota(jnp.int32, (LANES, LANES), 1)
    lower = jnp.where(row_id >= lane_id, 1.0, 0.0).astype(BF16)
    upper = jnp.where(row_id < lane_id, 1.0, 0.0).astype(BF16)
    return lower, upper


def frame_pairs(xs, pr, rows):
    tri = jnp.concatenate(triangles(), axis=1)
    ones_band = jnp.concatenate([tri, tri], axis=0)
    pair = jnp.concatenate([xs[pl.ds(0, rows), :], xs[pl.ds(1, rows), :]], axis=1)
    square = pair * pair
    high = square.astype(BF16)
    low = (square - high.astype(F32)).astype(BF16)
    both = jnp.dot(high, ones_band, preferred_element_type=F32) + jnp.dot(
        low, ones_band, preferred_element_type=F32
    )
    pr[pl.ds(0, rows), :] = both[:, LANES:]
    pr[pl.ds(rows, 8), :] = jnp.zeros((8, LANES), F32)
    return pair.astype(BF16), both[:, :LANES] + pr[pl.ds(1, rows), :]


def frame_kernel(rec, right, xx, ee, xs, pr):
    for b in range(12):
        part, at = (rec, b) if b < 8 else (right, b - 8)
        xs[pl.ds(b, CH, stride=ROWS), :] = part[:, LANES * at : LANES * (at + 1)].astype(F32)
    for b in range(12, ROWS):
        xs[pl.ds(b, CH, stride=ROWS), :] = jnp.zeros((CH, LANES), F32)
    xs[pl.ds(CH * ROWS, 8), :] = jnp.zeros((8, LANES), F32)
    xx[...], ee[...] = frame_pairs(xs, pr, CH * ROWS)


def own_slots(k):
    return min(SLOTS, max(0, CH - 5 - 3 * k))


def stacked(table, k, slots, first_row, total_chan, xx, ee, wr, we, sh):
    group = lax.axis_index("chan")
    lower, upper = triangles()
    lane_row = lax.broadcasted_iota(jnp.int32, (TPL, LANES), 1)

    def circulant(p, half):
        row = wr[half, pl.ds(p, 1), :]
        full = jnp.broadcast_to(row, (LANES, LANES)).astype(BF16)
        return pltpu.roll(full, 1, 1, stride=1, stride_axis=0)

    total = jnp.zeros((TPL, LANES), F32)
    for j in slots:
        p = j * TPL + k
        listed = table[k, j]
        valid = listed >= 0
        place = listed - group * CH
        place = jnp.where(place < 0, place + total_chan, place) - first_row
        place = jnp.where(valid, place, 0)
        start = pl.multiple_of(place * ROWS, ROWS)
        shift = table[k, SLOTS + j]
        lanes, rows = shift & (LANES - 1), shift >> 7
        first, second = circulant(p, 0), circulant(p, 1)
        band = jnp.concatenate(
            [
                jnp.concatenate([first * lower, first * upper], axis=1),
                jnp.concatenate([second * lower, second * upper], axis=1),
            ],
            axis=0,
        )
        prod = jnp.dot(xx[pl.ds(start, ROWS), :], band, preferred_element_type=F32)
        corr = prod[:, :LANES] + pltpu.roll(prod[:, LANES:], ROWS - 1, 0)
        scale = we[pl.ds(p, 1), :] * ee[pl.ds(start, ROWS), :] + 1e-06
        normed = corr * lax.rsqrt(scale)
        sh[j] = pltpu.roll(normed, (LANES - lanes) & (LANES - 1), 1)
        here = sh[j, pl.ds(rows, TPL), :]
        after = sh[j, pl.ds(rows + 1, TPL), :]
        moved = jnp.where(lane_row < LANES - lanes, here, after)
        total = total + jnp.where(valid, moved, 0.0)
    return total


def own_kernel(total_chan, table_v, xx, ee, waves, part, wr, we, sh, table, sem):
    copy = pltpu.make_async_copy(table_v, table, sem)
    copy.start()
    order = [h + i for h in (0, LANES) for i in reversed(range(0, LANES, ROWS))]
    wave_t = jnp.concatenate([waves[pl.ds(RING.index(i // ROWS) * ROWS, ROWS), :].astype(F32) for i in order], axis=0).T
    wr[0] = wave_t[:, :LANES]
    wr[1] = wave_t[:, LANES:]
    we[...] = jnp.broadcast_to(jnp.sum(wave_t * wave_t, axis=1, keepdims=True), we.shape)
    copy.wait()
    for k in range(TPL):
        part[k] = stacked(table, k, range(own_slots(k)), 0, total_chan, xx, ee, wr, we, sh)


def rest_kernel(total_chan, table_v, own_xx, own_ee, below, part, wr, we, out, xs, pr, xx, ee, sh, table, sem):
    copy = pltpu.make_async_copy(table_v, table, sem)
    copy.start()
    for b in range(12):
        xs[pl.ds(b, SPILL, stride=ROWS), :] = below[:, LANES * b : LANES * (b + 1)].astype(F32)
    for b in range(12, ROWS):
        xs[pl.ds(b, SPILL, stride=ROWS), :] = jnp.zeros((SPILL, LANES), F32)
    xs[pl.ds(SPILL * ROWS, 8), :] = jnp.zeros((8, LANES), F32)
    kept = (CH - FROM) * ROWS
    xx[pl.ds(0, kept), :] = own_xx[pl.ds(FROM * ROWS, kept), :]
    ee[pl.ds(0, kept), :] = own_ee[pl.ds(FROM * ROWS, kept), :]
    pairs, energy = frame_pairs(xs, pr, SPILL * ROWS)
    xx[pl.ds(kept, SPILL * ROWS), :] = pairs
    ee[pl.ds(kept, SPILL * ROWS), :] = energy

    out[...] = jnp.zeros_like(out)
    copy.wait()
    for k in range(TPL):
        slots = range(own_slots(k), SLOTS)
        total = part[k] + stacked(table, k, slots, FROM, total_chan, xx, ee, wr, we, sh)
        owner = table[k, 2 * SLOTS]
        rank = jnp.int32(0)
        for q in range(k):
            rank = rank + jnp.where(table[q, 2 * SLOTS] == owner, 1, 0)
        out[(out.shape[0] // SCAP - 1 - owner) * SCAP + rank] = total


def shifted(value, axis, count):
    return lax.ppermute(value, axis, [(s, (s - 1) % count) for s in range(count)])


def gathered(chunks):
    return lax.all_to_all(chunks, "tm", 0, 0, axis_index_groups=[RING]).reshape(L, LANES)


def local(records, template_waves, channel_lists, moveouts, owner_map):
    ch_dev, t_dev = records.shape
    n_chan = lax.axis_size("chan")
    n_tm = lax.axis_size("tm")
    vmem = pl.BlockSpec(memory_space=pltpu.VMEM)
    params = pltpu.CompilerParams(vmem_limit_bytes=24 * 1024 * 1024)

    chunks = pl.pallas_call(
        chunk_kernel,
        out_shape=jax.ShapeDtypeStruct((n_tm, L // n_tm, LANES), BF16),
        in_specs=[vmem],
        out_specs=vmem,
        compiler_params=params,
    )(jnp.transpose(template_waves, (1, 0, 2)))
    right = shifted(records, "tm", n_tm)
    edge = jnp.concatenate([records[:SPILL], right[:SPILL, :HALO]], axis=1)
    below = shifted(edge, "chan", n_chan)
    waves = gathered(chunks)
    scalars = [pltpu.SMEM((TPL, 2 * SLOTS + 1), jnp.int32), pltpu.SemaphoreType.DMA]

    def scratch(*shape):
        return pltpu.VMEM(shape, F32)

    frames, energy = pl.pallas_call(
        frame_kernel,
        out_shape=(
            jax.ShapeDtypeStruct((CH * ROWS, 2 * LANES), BF16),
            jax.ShapeDtypeStruct((CH * ROWS, LANES), F32),
        ),
        in_specs=[vmem] * 2,
        out_specs=(vmem, vmem),
        scratch_shapes=[scratch(CH * ROWS + 8, LANES)] * 2,
        compiler_params=params,
        cost_estimate=pl.CostEstimate(flops=200_000_000, bytes_accessed=1_000_000, transcendentals=0),
    )(records, right)
    lists, shifts, owners, energy = lax.optimization_barrier((channel_lists, moveouts, owner_map, energy))
    table = jnp.concatenate([lists, shifts, owners], axis=1)
    table = lax.dynamic_slice_in_dim(table, lax.axis_index("chan") * TPL, TPL, 0)
    part, rows_w, energy_w = pl.pallas_call(
        lambda *refs: own_kernel(ch_dev * n_chan, *refs),
        out_shape=(
            jax.ShapeDtypeStruct((TPL, TPL, LANES), F32),
            jax.ShapeDtypeStruct((2, LANES, LANES), F32),
            jax.ShapeDtypeStruct((LANES, LANES), F32),
        ),
        in_specs=[vmem] * 4,
        out_specs=(vmem,) * 3,
        scratch_shapes=[scratch(SLOTS, ROWS, LANES)] + scalars,
        compiler_params=params,
        cost_estimate=pl.CostEstimate(flops=1_000_000_000, bytes_accessed=1_000_000, transcendentals=0),
    )(table, frames, energy, waves)
    late_rows = (CH - FROM + SPILL) * ROWS
    outgoing = pl.pallas_call(
        lambda *refs: rest_kernel(ch_dev * n_chan, *refs),
        out_shape=jax.ShapeDtypeStruct((n_chan * SCAP, TPL, LANES), F32),
        in_specs=[vmem] * 7,
        out_specs=vmem,
        scratch_shapes=[
            scratch(SPILL * ROWS + 8, LANES),
            scratch(SPILL * ROWS + 8, LANES),
            pltpu.VMEM((late_rows, 2 * LANES), BF16),
            scratch(late_rows, LANES),
            scratch(SLOTS, ROWS, LANES),
        ]
        + scalars,
        compiler_params=params,
    )(table, frames, energy, below, part, rows_w, energy_w)
    incoming = lax.all_to_all(
        outgoing.reshape(n_chan, SCAP, TPL, LANES),
        "chan",
        0,
        0,
        axis_index_groups=[list(reversed(range(n_chan)))],
    )[::-1]
    return incoming.reshape(n_chan * SCAP, t_dev)


def solution(mesh):
    in_specs = (P("chan", "tm"), P("chan", None, "tm"), P(), P(), P())
    out_specs = P("chan", "tm")
    return jax.shard_map(local, mesh=mesh, in_specs=in_specs, out_specs=out_specs, check_vma=False)
```

```python
import jax
import jax.numpy as jnp
from jax import lax
from jax.experimental import pallas as pl
from jax.experimental.pallas import tpu as pltpu
from jax.sharding import PartitionSpec as P

L = 256
SLOTS = 12
SPILL = 16
LANES = 128
ROWS = 16
HALO = 512
TPL = 8
CH = 24
SCAP = 2
PAIRS = TPL * SLOTS
FROM = 16
RING = [(15 - i) % 16 for i in range(16)]
F32 = jnp.float32
BF16 = jnp.bfloat16


def chunk_kernel(waves, out):
    rows = [waves[j].astype(F32) for j in range(SLOTS)]
    flat = jnp.concatenate(rows + [jnp.zeros((LANES - PAIRS, rows[0].shape[1]), F32)], axis=0)
    wide = jnp.concatenate([flat, jnp.zeros((LANES, LANES - flat.shape[1]), F32)], axis=1)
    turned = wide.T[: out.shape[1]]
    last = out.shape[1] - 1
    turned = jnp.concatenate([turned[last - i : last - i + 1] for i in range(last + 1)], axis=0).astype(BF16)
    for i in range(out.shape[0]):
        out[i] = turned


def triangles():
    row_id = lax.broadcasted_iota(jnp.int32, (LANES, LANES), 0)
    lane_id = lax.broadcasted_iota(jnp.int32, (LANES, LANES), 1)
    lower = jnp.where(row_id >= lane_id, 1.0, 0.0).astype(BF16)
    upper = jnp.where(row_id < lane_id, 1.0, 0.0).astype(BF16)
    return lower, upper


def frame_pairs(xs, pr, rows):
    tri = jnp.concatenate(triangles(), axis=1)
    ones_band = jnp.concatenate([tri, tri], axis=0)
    pair = jnp.concatenate([xs[pl.ds(0, rows), :], xs[pl.ds(1, rows), :]], axis=1)
    square = pair * pair
    high = square.astype(BF16)
    low = (square - high.astype(F32)).astype(BF16)
    both = jnp.dot(high, ones_band, preferred_element_type=F32) + jnp.dot(
        low, ones_band, preferred_element_type=F32
    )
    pr[pl.ds(0, rows), :] = both[:, LANES:]
    pr[pl.ds(rows, 8), :] = jnp.zeros((8, LANES), F32)
    return pair.astype(BF16), both[:, :LANES] + pr[pl.ds(1, rows), :]


def frame_kernel(rec, right, owners, xx, ee, held, xs, pr):
    for b in range(12):
        part, at = (rec, b) if b < 8 else (right, b - 8)
        xs[pl.ds(b, CH, stride=ROWS), :] = part[:, LANES * at : LANES * (at + 1)].astype(F32)
    for b in range(12, ROWS):
        xs[pl.ds(b, CH, stride=ROWS), :] = jnp.zeros((CH, LANES), F32)
    xs[pl.ds(CH * ROWS, 8), :] = jnp.zeros((8, LANES), F32)
    xx[...], ee[...] = frame_pairs(xs, pr, CH * ROWS)
    held[...] = owners[...]


def own_slots(k):
    return min(SLOTS, max(0, CH - 5 - 3 * k))


def stacked(table, k, slots, first_row, total_chan, xx, ee, wr, we, sh):
    group = lax.axis_index("chan")
    lower, upper = triangles()
    lane_row = lax.broadcasted_iota(jnp.int32, (TPL, LANES), 1)

    def circulant(p, half):
        row = wr[half, pl.ds(p, 1), :]
        full = jnp.broadcast_to(row, (LANES, LANES)).astype(BF16)
        return pltpu.roll(full, 1, 1, stride=1, stride_axis=0)

    total = jnp.zeros((TPL, LANES), F32)
    for j in slots:
        p = j * TPL + k
        listed = table[k, j]
        valid = listed >= 0
        place = listed - group * CH
        place = jnp.where(place < 0, place + total_chan, place) - first_row
        place = jnp.where(valid, place, 0)
        start = pl.multiple_of(place * ROWS, ROWS)
        shift = table[k, SLOTS + j]
        lanes, rows = shift & (LANES - 1), shift >> 7
        first, second = circulant(p, 0), circulant(p, 1)
        band = jnp.concatenate(
            [
                jnp.concatenate([first * lower, first * upper], axis=1),
                jnp.concatenate([second * lower, second * upper], axis=1),
            ],
            axis=0,
        )
        prod = jnp.dot(xx[pl.ds(start, ROWS), :], band, preferred_element_type=F32)
        corr = prod[:, :LANES] + pltpu.roll(prod[:, LANES:], ROWS - 1, 0)
        scale = we[pl.ds(p, 1), :] * ee[pl.ds(start, ROWS), :] + 1e-06
        normed = corr * lax.rsqrt(scale)
        sh[j] = pltpu.roll(normed, (LANES - lanes) & (LANES - 1), 1)
        here = sh[j, pl.ds(rows, TPL), :]
        after = sh[j, pl.ds(rows + 1, TPL), :]
        moved = jnp.where(lane_row < LANES - lanes, here, after)
        total = total + jnp.where(valid, moved, 0.0)
    return total


def own_kernel(total_chan, table_v, xx, ee, waves, part, wr, we, sh, table, sem):
    copy = pltpu.make_async_copy(table_v, table, sem)
    copy.start()
    order = [h + i for h in (0, LANES) for i in reversed(range(0, LANES, ROWS))]
    wave_t = jnp.concatenate([waves[pl.ds(RING.index(i // ROWS) * ROWS, ROWS), :].astype(F32) for i in order], axis=0).T
    wr[0] = wave_t[:, :LANES]
    wr[1] = wave_t[:, LANES:]
    we[...] = jnp.broadcast_to(jnp.sum(wave_t * wave_t, axis=1, keepdims=True), we.shape)
    copy.wait()
    for k in range(TPL):
        part[k] = stacked(table, k, range(own_slots(k)), 0, total_chan, xx, ee, wr, we, sh)


def rest_kernel(total_chan, table_v, owners_v, own_xx, own_ee, below, part, wr, we, out, xs, pr, xx, ee, sh, table, sem, owners, owner_sem):
    copy = pltpu.make_async_copy(table_v, table, sem)
    copy.start()
    owner_copy = pltpu.make_async_copy(owners_v, owners, owner_sem)
    owner_copy.start()
    for b in range(12):
        xs[pl.ds(b, SPILL, stride=ROWS), :] = below[:, LANES * b : LANES * (b + 1)].astype(F32)
    for b in range(12, ROWS):
        xs[pl.ds(b, SPILL, stride=ROWS), :] = jnp.zeros((SPILL, LANES), F32)
    xs[pl.ds(SPILL * ROWS, 8), :] = jnp.zeros((8, LANES), F32)
    kept = (CH - FROM) * ROWS
    xx[pl.ds(0, kept), :] = own_xx[pl.ds(FROM * ROWS, kept), :]
    ee[pl.ds(0, kept), :] = own_ee[pl.ds(FROM * ROWS, kept), :]
    pairs, energy = frame_pairs(xs, pr, SPILL * ROWS)
    xx[pl.ds(kept, SPILL * ROWS), :] = pairs
    ee[pl.ds(kept, SPILL * ROWS), :] = energy

    out[...] = jnp.zeros_like(out)
    copy.wait()
    owner_copy.wait()
    first = lax.axis_index("chan") * TPL
    for k in range(TPL):
        slots = range(own_slots(k), SLOTS)
        total = part[k] + stacked(table, k, slots, FROM, total_chan, xx, ee, wr, we, sh)
        owner = owners[0, first + k]
        rank = jnp.int32(0)
        for q in range(k):
            rank = rank + jnp.where(owners[0, first + q] == owner, 1, 0)
        out[(out.shape[0] // SCAP - 1 - owner) * SCAP + rank] = total


def shifted(value, axis, count):
    return lax.ppermute(value, axis, [(s, (s - 1) % count) for s in range(count)])


def gathered(chunks):
    return lax.all_to_all(chunks, "tm", 0, 0, axis_index_groups=[RING]).reshape(L, LANES)


def local(records, template_waves, channel_lists, moveouts, owner_map):
    ch_dev, t_dev = records.shape
    n_chan = lax.axis_size("chan")
    n_tm = lax.axis_size("tm")
    vmem = pl.BlockSpec(memory_space=pltpu.VMEM)
    params = pltpu.CompilerParams(vmem_limit_bytes=24 * 1024 * 1024)

    chunks = pl.pallas_call(
        chunk_kernel,
        out_shape=jax.ShapeDtypeStruct((n_tm, L // n_tm, LANES), BF16),
        in_specs=[vmem],
        out_specs=vmem,
        compiler_params=params,
    )(jnp.transpose(template_waves, (1, 0, 2)))
    right = shifted(records, "tm", n_tm)
    edge = jnp.concatenate([records[:SPILL], right[:SPILL, :HALO]], axis=1)
    below = shifted(edge, "chan", n_chan)
    waves = gathered(chunks)
    scalars = [pltpu.SMEM((TPL, 2 * SLOTS), jnp.int32), pltpu.SemaphoreType.DMA]

    def scratch(*shape):
        return pltpu.VMEM(shape, F32)

    frames, energy, owners = pl.pallas_call(
        frame_kernel,
        out_shape=(
            jax.ShapeDtypeStruct((CH * ROWS, 2 * LANES), BF16),
            jax.ShapeDtypeStruct((CH * ROWS, LANES), F32),
            jax.ShapeDtypeStruct((1, owner_map.shape[0]), jnp.int32),
        ),
        in_specs=[vmem] * 3,
        out_specs=(vmem,) * 3,
        scratch_shapes=[scratch(CH * ROWS + 8, LANES)] * 2,
        compiler_params=params,
        cost_estimate=pl.CostEstimate(flops=200_000_000, bytes_accessed=1_000_000, transcendentals=0),
    )(records, right, owner_map.T)
    lists, shifts, energy = lax.optimization_barrier((channel_lists, moveouts, energy))
    table = jnp.concatenate([lists, shifts], axis=1)
    table = lax.dynamic_slice_in_dim(table, lax.axis_index("chan") * TPL, TPL, 0)
    part, rows_w, energy_w = pl.pallas_call(
        lambda *refs: own_kernel(ch_dev * n_chan, *refs),
        out_shape=(
            jax.ShapeDtypeStruct((TPL, TPL, LANES), F32),
            jax.ShapeDtypeStruct((2, LANES, LANES), F32),
            jax.ShapeDtypeStruct((LANES, LANES), F32),
        ),
        in_specs=[vmem] * 4,
        out_specs=(vmem,) * 3,
        scratch_shapes=[scratch(SLOTS, ROWS, LANES)] + scalars,
        compiler_params=params,
        cost_estimate=pl.CostEstimate(flops=1_000_000_000, bytes_accessed=1_000_000, transcendentals=0),
    )(table, frames, energy, waves)
    late_rows = (CH - FROM + SPILL) * ROWS
    outgoing = pl.pallas_call(
        lambda *refs: rest_kernel(ch_dev * n_chan, *refs),
        out_shape=jax.ShapeDtypeStruct((n_chan * SCAP, TPL, LANES), F32),
        in_specs=[vmem] * 8,
        out_specs=vmem,
        scratch_shapes=[
            scratch(SPILL * ROWS + 8, LANES),
            scratch(SPILL * ROWS + 8, LANES),
            pltpu.VMEM((late_rows, 2 * LANES), BF16),
            scratch(late_rows, LANES),
            scratch(SLOTS, ROWS, LANES),
        ]
        + scalars
        + [pltpu.SMEM((1, owner_map.shape[0]), jnp.int32), pltpu.SemaphoreType.DMA],
        compiler_params=params,
    )(table, owners, frames, energy, below, part, rows_w, energy_w)
    incoming = lax.all_to_all(
        outgoing.reshape(n_chan, SCAP, TPL, LANES),
        "chan",
        0,
        0,
        axis_index_groups=[list(reversed(range(n_chan)))],
    )[::-1]
    return incoming.reshape(n_chan * SCAP, t_dev)


def solution(mesh):
    in_specs = (P("chan", "tm"), P("chan", None, "tm"), P(), P(), P())
    out_specs = P("chan", "tm")
    return jax.shard_map(local, mesh=mesh, in_specs=in_specs, out_specs=out_specs, check_vma=False)
```

```python
import jax
import jax.numpy as jnp
from jax import lax
from jax.experimental import pallas as pl
from jax.experimental.pallas import tpu as pltpu
from jax.sharding import PartitionSpec as P

L = 256
SLOTS = 12
SPILL = 16
LANES = 128
ROWS = 16
HALO = 512
TPL = 8
CH = 24
SCAP = 2
PAIRS = TPL * SLOTS
FROM = 16
RING = [(15 - i) % 16 for i in range(16)]
F32 = jnp.float32
BF16 = jnp.bfloat16


def chunk_kernel(waves, out):
    rows = [waves[j].astype(F32) for j in range(SLOTS)]
    flat = jnp.concatenate(rows + [jnp.zeros((LANES - PAIRS, rows[0].shape[1]), F32)], axis=0)
    wide = jnp.concatenate([flat, jnp.zeros((LANES, LANES - flat.shape[1]), F32)], axis=1)
    turned = wide.T[: out.shape[1]]
    last = out.shape[1] - 1
    turned = jnp.concatenate([turned[last - i : last - i + 1] for i in range(last + 1)], axis=0).astype(BF16)
    for i in range(out.shape[0]):
        out[i] = turned


def triangles():
    row_id = lax.broadcasted_iota(jnp.int32, (LANES, LANES), 0)
    lane_id = lax.broadcasted_iota(jnp.int32, (LANES, LANES), 1)
    lower = jnp.where(row_id >= lane_id, 1.0, 0.0).astype(BF16)
    upper = jnp.where(row_id < lane_id, 1.0, 0.0).astype(BF16)
    return lower, upper


def frame_pairs(xs, pr, rows):
    tri = jnp.concatenate(triangles(), axis=1)
    ones_band = jnp.concatenate([tri, tri], axis=0)
    pair = jnp.concatenate([xs[pl.ds(0, rows), :], xs[pl.ds(1, rows), :]], axis=1)
    square = pair * pair
    high = square.astype(BF16)
    low = (square - high.astype(F32)).astype(BF16)
    both = jnp.dot(high, ones_band, preferred_element_type=F32) + jnp.dot(
        low, ones_band, preferred_element_type=F32
    )
    pr[pl.ds(0, rows), :] = both[:, LANES:]
    pr[pl.ds(rows, 8), :] = jnp.zeros((8, LANES), F32)
    return pair.astype(BF16), both[:, :LANES] + pr[pl.ds(1, rows), :]


def frame_kernel(rec, right, owners, lists, shifts, xx, ee, held, both, xs, pr):
    for b in range(12):
        part, at = (rec, b) if b < 8 else (right, b - 8)
        xs[pl.ds(b, CH, stride=ROWS), :] = part[:, LANES * at : LANES * (at + 1)].astype(F32)
    for b in range(12, ROWS):
        xs[pl.ds(b, CH, stride=ROWS), :] = jnp.zeros((CH, LANES), F32)
    xs[pl.ds(CH * ROWS, 8), :] = jnp.zeros((8, LANES), F32)
    xx[...], ee[...] = frame_pairs(xs, pr, CH * ROWS)
    held[...] = owners[...]
    both[pl.ds(0, SLOTS), :] = lists[...]
    both[pl.ds(ROWS, SLOTS), :] = shifts[...]
    both[pl.ds(SLOTS, ROWS - SLOTS), :] = jnp.zeros((ROWS - SLOTS, both.shape[1]), jnp.int32)
    both[pl.ds(ROWS + SLOTS, ROWS - SLOTS), :] = jnp.zeros((ROWS - SLOTS, both.shape[1]), jnp.int32)


def own_slots(k):
    return min(SLOTS, max(0, CH - 5 - 3 * k))


def stacked(table, k, slots, first_row, total_chan, xx, ee, wr, we, sh):
    group = lax.axis_index("chan")
    lower, upper = triangles()
    lane_row = lax.broadcasted_iota(jnp.int32, (TPL, LANES), 1)

    def circulant(p, half):
        row = wr[half, pl.ds(p, 1), :]
        full = jnp.broadcast_to(row, (LANES, LANES)).astype(BF16)
        return pltpu.roll(full, 1, 1, stride=1, stride_axis=0)

    total = jnp.zeros((TPL, LANES), F32)
    for j in slots:
        p = j * TPL + k
        listed = table[k, j]
        valid = listed >= 0
        place = listed - group * CH
        place = jnp.where(place < 0, place + total_chan, place) - first_row
        place = jnp.where(valid, place, 0)
        start = pl.multiple_of(place * ROWS, ROWS)
        shift = table[k, ROWS + j]
        lanes, rows = shift & (LANES - 1), shift >> 7
        first, second = circulant(p, 0), circulant(p, 1)
        band = jnp.concatenate(
            [
                jnp.concatenate([first * lower, first * upper], axis=1),
                jnp.concatenate([second * lower, second * upper], axis=1),
            ],
            axis=0,
        )
        prod = jnp.dot(xx[pl.ds(start, ROWS), :], band, preferred_element_type=F32)
        corr = prod[:, :LANES] + pltpu.roll(prod[:, LANES:], ROWS - 1, 0)
        scale = we[pl.ds(p, 1), :] * ee[pl.ds(start, ROWS), :] + 1e-06
        normed = corr * lax.rsqrt(scale)
        sh[j] = pltpu.roll(normed, (LANES - lanes) & (LANES - 1), 1)
        here = sh[j, pl.ds(rows, TPL), :]
        after = sh[j, pl.ds(rows + 1, TPL), :]
        moved = jnp.where(lane_row < LANES - lanes, here, after)
        total = total + jnp.where(valid, moved, 0.0)
    return total


def own_kernel(total_chan, table_v, xx, ee, waves, part, wr, we, sh, table, sem):
    copy = pltpu.make_async_copy(table_v, table, sem)
    copy.start()
    order = [h + i for h in (0, LANES) for i in reversed(range(0, LANES, ROWS))]
    wave_t = jnp.concatenate([waves[pl.ds(RING.index(i // ROWS) * ROWS, ROWS), :].astype(F32) for i in order], axis=0).T
    wr[0] = wave_t[:, :LANES]
    wr[1] = wave_t[:, LANES:]
    we[...] = jnp.broadcast_to(jnp.sum(wave_t * wave_t, axis=1, keepdims=True), we.shape)
    copy.wait()
    for k in range(TPL):
        part[k] = stacked(table, k, range(own_slots(k)), 0, total_chan, xx, ee, wr, we, sh)


def rest_kernel(total_chan, table_v, owners_v, own_xx, own_ee, below, part, wr, we, out, xs, pr, xx, ee, sh, table, sem, owners, owner_sem):
    copy = pltpu.make_async_copy(table_v, table, sem)
    copy.start()
    owner_copy = pltpu.make_async_copy(owners_v, owners, owner_sem)
    owner_copy.start()
    for b in range(12):
        xs[pl.ds(b, SPILL, stride=ROWS), :] = below[:, LANES * b : LANES * (b + 1)].astype(F32)
    for b in range(12, ROWS):
        xs[pl.ds(b, SPILL, stride=ROWS), :] = jnp.zeros((SPILL, LANES), F32)
    xs[pl.ds(SPILL * ROWS, 8), :] = jnp.zeros((8, LANES), F32)
    kept = (CH - FROM) * ROWS
    xx[pl.ds(0, kept), :] = own_xx[pl.ds(FROM * ROWS, kept), :]
    ee[pl.ds(0, kept), :] = own_ee[pl.ds(FROM * ROWS, kept), :]
    pairs, energy = frame_pairs(xs, pr, SPILL * ROWS)
    xx[pl.ds(kept, SPILL * ROWS), :] = pairs
    ee[pl.ds(kept, SPILL * ROWS), :] = energy

    out[...] = jnp.zeros_like(out)
    copy.wait()
    owner_copy.wait()
    first = lax.axis_index("chan") * TPL
    for k in range(TPL):
        slots = range(own_slots(k), SLOTS)
        total = part[k] + stacked(table, k, slots, FROM, total_chan, xx, ee, wr, we, sh)
        owner = owners[0, first + k]
        rank = jnp.int32(0)
        for q in range(k):
            rank = rank + jnp.where(owners[0, first + q] == owner, 1, 0)
        out[(out.shape[0] // SCAP - 1 - owner) * SCAP + rank] = total


def shifted(value, axis, count):
    return lax.ppermute(value, axis, [(s, (s - 1) % count) for s in range(count)])


def gathered(chunks):
    return lax.all_to_all(chunks, "tm", 0, 0, axis_index_groups=[RING]).reshape(L, LANES)


def local(records, template_waves, channel_lists, moveouts, owner_map):
    ch_dev, t_dev = records.shape
    n_chan = lax.axis_size("chan")
    n_tm = lax.axis_size("tm")
    vmem = pl.BlockSpec(memory_space=pltpu.VMEM)
    params = pltpu.CompilerParams(vmem_limit_bytes=24 * 1024 * 1024)

    chunks = pl.pallas_call(
        chunk_kernel,
        out_shape=jax.ShapeDtypeStruct((n_tm, L // n_tm, LANES), BF16),
        in_specs=[vmem],
        out_specs=vmem,
        compiler_params=params,
    )(jnp.transpose(template_waves, (1, 0, 2)))
    right = shifted(records, "tm", n_tm)
    edge = jnp.concatenate([records[:SPILL], right[:SPILL, :HALO]], axis=1)
    below = shifted(edge, "chan", n_chan)
    waves = gathered(chunks)
    scalars = [pltpu.SMEM((TPL, 2 * ROWS), jnp.int32), pltpu.SemaphoreType.DMA]

    def scratch(*shape):
        return pltpu.VMEM(shape, F32)

    frames, energy, owners, both = pl.pallas_call(
        frame_kernel,
        out_shape=(
            jax.ShapeDtypeStruct((CH * ROWS, 2 * LANES), BF16),
            jax.ShapeDtypeStruct((CH * ROWS, LANES), F32),
            jax.ShapeDtypeStruct((1, owner_map.shape[0]), jnp.int32),
            jax.ShapeDtypeStruct((2 * ROWS, owner_map.shape[0]), jnp.int32),
        ),
        in_specs=[vmem] * 5,
        out_specs=(vmem,) * 4,
        scratch_shapes=[scratch(CH * ROWS + 8, LANES)] * 2,
        compiler_params=params,
        cost_estimate=pl.CostEstimate(flops=200_000_000, bytes_accessed=1_000_000, transcendentals=0),
    )(records, right, owner_map.T, channel_lists.T, moveouts.T)
    table = lax.dynamic_slice_in_dim(both, lax.axis_index("chan") * TPL, TPL, 1).T
    part, rows_w, energy_w = pl.pallas_call(
        lambda *refs: own_kernel(ch_dev * n_chan, *refs),
        out_shape=(
            jax.ShapeDtypeStruct((TPL, TPL, LANES), F32),
            jax.ShapeDtypeStruct((2, LANES, LANES), F32),
            jax.ShapeDtypeStruct((LANES, LANES), F32),
        ),
        in_specs=[vmem] * 4,
        out_specs=(vmem,) * 3,
        scratch_shapes=[scratch(SLOTS, ROWS, LANES)] + scalars,
        compiler_params=params,
        cost_estimate=pl.CostEstimate(flops=1_000_000_000, bytes_accessed=1_000_000, transcendentals=0),
    )(table, frames, energy, waves)
    late_rows = (CH - FROM + SPILL) * ROWS
    outgoing = pl.pallas_call(
        lambda *refs: rest_kernel(ch_dev * n_chan, *refs),
        out_shape=jax.ShapeDtypeStruct((n_chan * SCAP, TPL, LANES), F32),
        in_specs=[vmem] * 8,
        out_specs=vmem,
        scratch_shapes=[
            scratch(SPILL * ROWS + 8, LANES),
            scratch(SPILL * ROWS + 8, LANES),
            pltpu.VMEM((late_rows, 2 * LANES), BF16),
            scratch(late_rows, LANES),
            scratch(SLOTS, ROWS, LANES),
        ]
        + scalars
        + [pltpu.SMEM((1, owner_map.shape[0]), jnp.int32), pltpu.SemaphoreType.DMA],
        compiler_params=params,
    )(table, owners, frames, energy, below, part, rows_w, energy_w)
    incoming = lax.all_to_all(
        outgoing.reshape(n_chan, SCAP, TPL, LANES),
        "chan",
        0,
        0,
        axis_index_groups=[list(reversed(range(n_chan)))],
    )[::-1]
    return incoming.reshape(n_chan * SCAP, t_dev)


def solution(mesh):
    in_specs = (P("chan", "tm"), P("chan", None, "tm"), P(), P(), P())
    out_specs = P("chan", "tm")
    return jax.shard_map(local, mesh=mesh, in_specs=in_specs, out_specs=out_specs, check_vma=False)
```

```python
import jax
import jax.numpy as jnp
from jax import lax
from jax.experimental import pallas as pl
from jax.experimental.pallas import tpu as pltpu
from jax.sharding import PartitionSpec as P

L = 256
SLOTS = 12
SPILL = 16
LANES = 128
ROWS = 16
HALO = 512
TPL = 8
CH = 24
SCAP = 2
PAIRS = TPL * SLOTS
FROM = 19
RING = [(15 - i) % 16 for i in range(16)]
F32 = jnp.float32
BF16 = jnp.bfloat16


def chunk_kernel(waves, out):
    rows = [waves[j].astype(F32) for j in range(SLOTS)]
    flat = jnp.concatenate(rows + [jnp.zeros((LANES - PAIRS, rows[0].shape[1]), F32)], axis=0)
    wide = jnp.concatenate([flat, jnp.zeros((LANES, LANES - flat.shape[1]), F32)], axis=1)
    turned = wide.T[: out.shape[1]]
    last = out.shape[1] - 1
    turned = jnp.concatenate([turned[last - i : last - i + 1] for i in range(last + 1)], axis=0).astype(BF16)
    for i in range(out.shape[0]):
        out[i] = turned


def triangles():
    row_id = lax.broadcasted_iota(jnp.int32, (LANES, LANES), 0)
    lane_id = lax.broadcasted_iota(jnp.int32, (LANES, LANES), 1)
    lower = jnp.where(row_id >= lane_id, 1.0, 0.0).astype(BF16)
    upper = jnp.where(row_id < lane_id, 1.0, 0.0).astype(BF16)
    return lower, upper


def frame_pairs(xs, pr, rows):
    tri = jnp.concatenate(triangles(), axis=1)
    ones_band = jnp.concatenate([tri, tri], axis=0)
    pair = jnp.concatenate([xs[pl.ds(0, rows), :], xs[pl.ds(1, rows), :]], axis=1)
    square = pair * pair
    high = square.astype(BF16)
    low = (square - high.astype(F32)).astype(BF16)
    both = jnp.dot(high, ones_band, preferred_element_type=F32) + jnp.dot(
        low, ones_band, preferred_element_type=F32
    )
    pr[pl.ds(0, rows), :] = both[:, LANES:]
    pr[pl.ds(rows, 8), :] = jnp.zeros((8, LANES), F32)
    return pair.astype(BF16), both[:, :LANES] + pr[pl.ds(1, rows), :]


def frame_kernel(rec, right, owners, xx, ee, held, xs, pr):
    for b in range(12):
        part, at = (rec, b) if b < 8 else (right, b - 8)
        xs[pl.ds(b, CH, stride=ROWS), :] = part[:, LANES * at : LANES * (at + 1)].astype(F32)
    for b in range(12, ROWS):
        xs[pl.ds(b, CH, stride=ROWS), :] = jnp.zeros((CH, LANES), F32)
    xs[pl.ds(CH * ROWS, 8), :] = jnp.zeros((8, LANES), F32)
    xx[...], ee[...] = frame_pairs(xs, pr, CH * ROWS)
    held[...] = owners[...]


def own_slots(k):
    return min(SLOTS, max(0, CH - 5 - 3 * k))


def stacked(table, k, slots, first_row, total_chan, xx, ee, wr, we, sh):
    group = lax.axis_index("chan")
    lower, upper = triangles()
    lane_row = lax.broadcasted_iota(jnp.int32, (TPL, LANES), 1)

    def circulant(p, half):
        row = wr[half, pl.ds(p, 1), :]
        full = jnp.broadcast_to(row, (LANES, LANES)).astype(BF16)
        return pltpu.roll(full, 1, 1, stride=1, stride_axis=0)

    total = jnp.zeros((TPL, LANES), F32)
    for j in slots:
        p = j * TPL + k
        listed = table[k, j]
        valid = listed >= 0
        place = listed - group * CH
        place = jnp.where(place < 0, place + total_chan, place) - first_row
        place = jnp.where(valid, place, 0)
        start = pl.multiple_of(place * ROWS, ROWS)
        shift = table[k, SLOTS + j]
        lanes, rows = shift & (LANES - 1), shift >> 7
        first, second = circulant(p, 0), circulant(p, 1)
        band = jnp.concatenate(
            [
                jnp.concatenate([first * lower, first * upper], axis=1),
                jnp.concatenate([second * lower, second * upper], axis=1),
            ],
            axis=0,
        )
        prod = jnp.dot(xx[pl.ds(start, ROWS), :], band, preferred_element_type=F32)
        corr = prod[:, :LANES] + pltpu.roll(prod[:, LANES:], ROWS - 1, 0)
        scale = we[pl.ds(p, 1), :] * ee[pl.ds(start, ROWS), :] + 1e-06
        normed = corr * lax.rsqrt(scale)
        sh[j] = pltpu.roll(normed, (LANES - lanes) & (LANES - 1), 1)
        here = sh[j, pl.ds(rows, TPL), :]
        after = sh[j, pl.ds(rows + 1, TPL), :]
        moved = jnp.where(lane_row < LANES - lanes, here, after)
        total = total + jnp.where(valid, moved, 0.0)
    return total


def own_kernel(total_chan, table_v, xx, ee, waves, part, wr, we, sh, table, sem):
    copy = pltpu.make_async_copy(table_v, table, sem)
    copy.start()
    order = [h + i for h in (0, LANES) for i in reversed(range(0, LANES, ROWS))]
    wave_t = jnp.concatenate([waves[pl.ds(RING.index(i // ROWS) * ROWS, ROWS), :].astype(F32) for i in order], axis=0).T
    wr[0] = wave_t[:, :LANES]
    wr[1] = wave_t[:, LANES:]
    we[...] = jnp.broadcast_to(jnp.sum(wave_t * wave_t, axis=1, keepdims=True), we.shape)
    copy.wait()
    for k in range(TPL):
        part[k] = stacked(table, k, range(own_slots(k)), 0, total_chan, xx, ee, wr, we, sh)


def rest_kernel(total_chan, table_v, owners_v, own_xx, own_ee, below, part, wr, we, out, xs, pr, xx, ee, sh, table, sem, owners, owner_sem):
    copy = pltpu.make_async_copy(table_v, table, sem)
    copy.start()
    owner_copy = pltpu.make_async_copy(owners_v, owners, owner_sem)
    owner_copy.start()
    for b in range(12):
        xs[pl.ds(b, SPILL, stride=ROWS), :] = below[:, LANES * b : LANES * (b + 1)].astype(F32)
    for b in range(12, ROWS):
        xs[pl.ds(b, SPILL, stride=ROWS), :] = jnp.zeros((SPILL, LANES), F32)
    xs[pl.ds(SPILL * ROWS, 8), :] = jnp.zeros((8, LANES), F32)
    kept = (CH - FROM) * ROWS
    xx[pl.ds(0, kept), :] = own_xx[pl.ds(FROM * ROWS, kept), :]
    ee[pl.ds(0, kept), :] = own_ee[pl.ds(FROM * ROWS, kept), :]
    pairs, energy = frame_pairs(xs, pr, SPILL * ROWS)
    xx[pl.ds(kept, SPILL * ROWS), :] = pairs
    ee[pl.ds(kept, SPILL * ROWS), :] = energy

    out[...] = jnp.zeros_like(out)
    copy.wait()
    owner_copy.wait()
    first = lax.axis_index("chan") * TPL
    for k in range(TPL):
        slots = range(own_slots(k), SLOTS)
        total = part[k] + stacked(table, k, slots, FROM, total_chan, xx, ee, wr, we, sh)
        owner = owners[0, first + k]
        rank = jnp.int32(0)
        for q in range(k):
            rank = rank + jnp.where(owners[0, first + q] == owner, 1, 0)
        out[(out.shape[0] // SCAP - 1 - owner) * SCAP + rank] = total


def shifted(value, axis, count):
    return lax.ppermute(value, axis, [(s, (s - 1) % count) for s in range(count)])


def gathered(chunks):
    return lax.all_to_all(chunks, "tm", 0, 0, axis_index_groups=[RING]).reshape(L, LANES)


def local(records, template_waves, channel_lists, moveouts, owner_map):
    ch_dev, t_dev = records.shape
    n_chan = lax.axis_size("chan")
    n_tm = lax.axis_size("tm")
    vmem = pl.BlockSpec(memory_space=pltpu.VMEM)
    params = pltpu.CompilerParams(vmem_limit_bytes=24 * 1024 * 1024)

    chunks = pl.pallas_call(
        chunk_kernel,
        out_shape=jax.ShapeDtypeStruct((n_tm, L // n_tm, LANES), BF16),
        in_specs=[vmem],
        out_specs=vmem,
        compiler_params=params,
    )(jnp.transpose(template_waves, (1, 0, 2)))
    right = shifted(records, "tm", n_tm)
    edge = jnp.concatenate([records[:SPILL], right[:SPILL, :HALO]], axis=1)
    below = shifted(edge, "chan", n_chan)
    waves = gathered(chunks)
    scalars = [pltpu.SMEM((TPL, 2 * SLOTS), jnp.int32), pltpu.SemaphoreType.DMA]

    def scratch(*shape):
        return pltpu.VMEM(shape, F32)

    frames, energy, owners = pl.pallas_call(
        frame_kernel,
        out_shape=(
            jax.ShapeDtypeStruct((CH * ROWS, 2 * LANES), BF16),
            jax.ShapeDtypeStruct((CH * ROWS, LANES), F32),
            jax.ShapeDtypeStruct((1, owner_map.shape[0]), jnp.int32),
        ),
        in_specs=[vmem] * 3,
        out_specs=(vmem,) * 3,
        scratch_shapes=[scratch(CH * ROWS + 8, LANES)] * 2,
        compiler_params=params,
        cost_estimate=pl.CostEstimate(flops=200_000_000, bytes_accessed=1_000_000, transcendentals=0),
    )(records, right, owner_map.T)
    lists, shifts, energy = lax.optimization_barrier((channel_lists, moveouts, energy))
    table = jnp.concatenate([lists, shifts], axis=1)
    table = lax.dynamic_slice_in_dim(table, lax.axis_index("chan") * TPL, TPL, 0)
    part, rows_w, energy_w = pl.pallas_call(
        lambda *refs: own_kernel(ch_dev * n_chan, *refs),
        out_shape=(
            jax.ShapeDtypeStruct((TPL, TPL, LANES), F32),
            jax.ShapeDtypeStruct((2, LANES, LANES), F32),
            jax.ShapeDtypeStruct((LANES, LANES), F32),
        ),
        in_specs=[vmem] * 4,
        out_specs=(vmem,) * 3,
        scratch_shapes=[scratch(SLOTS, ROWS, LANES)] + scalars,
        compiler_params=params,
        cost_estimate=pl.CostEstimate(flops=1_000_000_000, bytes_accessed=1_000_000, transcendentals=0),
    )(table, frames, energy, waves)
    late_rows = (CH - FROM + SPILL) * ROWS
    outgoing = pl.pallas_call(
        lambda *refs: rest_kernel(ch_dev * n_chan, *refs),
        out_shape=jax.ShapeDtypeStruct((n_chan * SCAP, TPL, LANES), F32),
        in_specs=[vmem] * 8,
        out_specs=vmem,
        scratch_shapes=[
            scratch(SPILL * ROWS + 8, LANES),
            scratch(SPILL * ROWS + 8, LANES),
            pltpu.VMEM((late_rows, 2 * LANES), BF16),
            scratch(late_rows, LANES),
            scratch(SLOTS, ROWS, LANES),
        ]
        + scalars
        + [pltpu.SMEM((1, owner_map.shape[0]), jnp.int32), pltpu.SemaphoreType.DMA],
        compiler_params=params,
    )(table, owners, frames, energy, below, part, rows_w, energy_w)
    incoming = lax.all_to_all(
        outgoing.reshape(n_chan, SCAP, TPL, LANES),
        "chan",
        0,
        0,
        axis_index_groups=[list(reversed(range(n_chan)))],
    )[::-1]
    return incoming.reshape(n_chan * SCAP, t_dev)


def solution(mesh):
    in_specs = (P("chan", "tm"), P("chan", None, "tm"), P(), P(), P())
    out_specs = P("chan", "tm")
    return jax.shard_map(local, mesh=mesh, in_specs=in_specs, out_specs=out_specs, check_vma=False)
```
